32 devices in a mesh: dp: 8 (over z, x), tensor: 4 (over y, core).
Axes of the slice: x: 2, y: 2, z: 4, core: 2. Of those that a mesh axis runs over, the one named last changes fastest.
Arguments:
- activations: bfloat16 [512, 24, 14336], P('dp', None, 'tensor'), may hold values from -6 to 6
- out_grads: bfloat16 [512, 24, 4096], P('dp', None, 'tensor'), may hold values from -6 to 6
- proj_in: bfloat16 [14336, 64], P('tensor'), may hold values from -0.046875 to 0.046875
- proj_out: bfloat16 [4096, 64], P('tensor'), may hold values from -0.09375 to 0.09375
- queries: bfloat16 [8, 2560, 4096], P('dp', 'tensor'), may hold values from -0.09375 to 0.09375
- candidates: int32 [512, 1], P('dp'), may hold values from 0 to 7; in each aligned block of 64 rows (0 to 63, 64 to 127, ...) at most 20 rows name the same one
Outputs:
- scores: float32 [512, 1, 2560], P('dp', None, 'tensor')
The draws below stay inside these ranges and needn't reach their ends.
Inputs may be any that keep to these rules, and one draw needn't show every extreme that they name: `candidates`: each example names 1 different groups. Among the 64 examples of one index of dp at most 20 name the same group, and in every draw some group is named by exactly 20 of them.
All inputs are finite; a program needn't handle non-finite values.
Results may differ from the reference program's by a relative error of at most 0.0029.
Values may be sent and summed in bfloat16 or wider, within the bound.
No kernel may reach another device: no remote copies, remote signals or barrier semaphores. Data moves between devices by JAX's collectives and lax.ppermute only.
A program may use at most 64 MiB of HBM per device.

```python
import math
import jax
import jax.numpy as jnp
import numpy as np
from jax import lax

D = 4096
FF = 14336
R = 64
T_EX = 24
EX_DEV = 64
GRAD = 4096
CANDS = 1
CAP = 20
EXAMPLES = 512
GROUPS = 8
QN = 2560
N_DP = 8


def level_of(rng, extent, pieces, smallest, largest):
    def one(axis_at, shards_of):
        heights = jax.random.uniform(jax.random.fold_in(jax.random.fold_in(rng, 6), axis_at), (shards_of,), jnp.float32, smallest / len(pieces), largest / len(pieces))
        return jnp.repeat(jnp.exp(heights), extent[axis_at] // shards_of).reshape((-1,) + (1,) * (len(extent) - axis_at - 1))

    gain = one(*pieces[0])
    for cut in pieces[1:]:
        gain = gain * one(*cut)
    return gain


def routed_block(own_key, own, number, rows, number_of, top, bound, skew):
    order = jax.random.permutation(own_key, number_of)
    packed, common = portions_of(number_of, rows * top, bound, skew, True), portions_of(number_of, rows * top, bound, skew, False)
    places = jnp.arange(number_of)

    def named(lengths, rotation):
        used = int((lengths > 0).sum())
        fixed = max(1, used // 4)
        moved = fixed + (places - fixed + rotation * (used - fixed)) % max(1, number_of - fixed)
        return jnp.zeros((number_of,), jnp.int32).at[order[jnp.where(places < fixed, places, moved)]].set(jnp.asarray(lengths, jnp.int32))

    lengths = jnp.where(number % 4 == 0, named(packed, number // 4), named(common, number - number // 4 - 1))
    mixed = jax.random.permutation(jax.random.fold_in(own, 3), number_of)
    donor, receiver = mixed[0:number_of // 2 * 2:2], mixed[1:number_of // 2 * 2:2]
    room = jnp.minimum(lengths[donor] - 1, bound - lengths[receiver]) // 2
    room = jnp.where((donor == order[0]) | (receiver == order[0]) | (lengths[receiver] == 0), 0, jnp.maximum(room, 0))
    moved = jax.random.randint(jax.random.fold_in(own, 4), (number_of // 2,), 0, 1 << 20) % (room + 1)
    lengths = lengths.at[donor].add(-moved).at[receiver].add(moved)
    members = jnp.searchsorted(jnp.cumsum(lengths), jnp.arange(rows * top), side="right").astype(jnp.int32)
    table = members.reshape(top, rows).T
    table = table[jax.random.permutation(jax.random.fold_in(own, 1), rows)]
    rotation = jax.random.randint(jax.random.fold_in(own, 2), (rows, 1), 0, top)
    return jnp.take_along_axis(table, (jnp.arange(top)[None, :] + rotation) % top, axis=1)


def portions_of(number_of, total, most, slope, full):
    weights = [(1 << 20) // math.isqrt(rank ** slope) + 1 for rank in range(1, number_of + 1)]
    largest = most if full else min(most, max(-(-total // number_of), total * weights[0] // sum(weights)))
    least = 1 if total - largest >= number_of - 1 else 0
    holding, surplus = [largest] + [least] * (number_of - 1), total - largest - least * (number_of - 1)
    while surplus > 0:
        movable = [i for i in range(1, number_of) if holding[i] < largest] or [i for i in range(1, number_of) if holding[i] < most]
        whole, remaining = sum([weights[i] for i in movable]), surplus
        for i in movable:
            addition = min(most - holding[i], max(1, remaining * weights[i] // whole), surplus)
            holding[i] = holding[i] + addition
            surplus = surplus - addition
    return np.array(holding)


def bell_draw(key, dims, spread, reach, pieces=(), held_as=jnp.bfloat16):
    level = level_of(key, dims, pieces, -0.22, 0.18) if pieces else 1.0
    entries = jax.random.normal(key, dims, jnp.float32) * spread * level
    return jnp.minimum(jnp.maximum(entries, -reach), reach).astype(held_as)


def setup_inputs(seed: int = 0) -> dict:
    splits = jax.random.split(jax.random.key(seed), 7)
    activations = bell_draw(splits[0], (EXAMPLES, T_EX, FF), 1.0, 6.0, ((0, 8), (2, 4)))
    out_grads = bell_draw(splits[1], (EXAMPLES, T_EX, D), 1.0, 6.0, ((0, 8), (2, 4)))
    proj_in = bell_draw(splits[2], (FF, R), FF ** -0.5, 0.046875, ((0, 4),))
    proj_out = bell_draw(splits[3], (D, R), D ** -0.5, 0.09375, ((0, 4),))
    queries = bell_draw(splits[4], (GROUPS, QN, GRAD), GRAD ** -0.5, 0.09375, ((0, 8), (1, 4)))
    candidates_keys = jax.random.split(jax.random.fold_in(splits[5], 1), EXAMPLES // EX_DEV)
    candidates_turns = jax.random.permutation(jax.random.fold_in(splits[5], 3), EXAMPLES // EX_DEV)
    candidates = jax.vmap(lambda own, number: routed_block(jax.random.fold_in(splits[5], 2), own, number, EX_DEV, N_DP, CANDS, CAP, 2))(candidates_keys, candidates_turns).reshape((EXAMPLES, CANDS))
    return {"activations": activations, "out_grads": out_grads, "proj_in": proj_in, "proj_out": proj_out, "queries": queries, "candidates": candidates}


epsilon = 1e-06

def reference(activations, out_grads, proj_in, proj_out, queries, candidates):
    row_count = EXAMPLES * T_EX
    act_proj = jnp.dot(activations.reshape(row_count, FF), proj_in, preferred_element_type=jnp.float32).reshape(EXAMPLES, T_EX, R)
    grad_proj = jnp.dot(out_grads.reshape(row_count, D), proj_out, preferred_element_type=jnp.float32).reshape(EXAMPLES, T_EX, R)
    example_grads = jnp.einsum('eta,etb->eab', grad_proj, act_proj, precision=lax.Precision.HIGHEST).reshape(EXAMPLES, GRAD)
    inv_rms = lax.rsqrt(lax.optimization_barrier(jnp.mean(example_grads * example_grads, axis=1, keepdims=True)) + epsilon)
    unit_grads = (example_grads * inv_rms).astype(jnp.bfloat16)
    flat_cands = candidates.reshape(-1).astype(jnp.int32)
    pair_count = EXAMPLES * CANDS
    sorted_pairs = jnp.argsort(flat_cands, stable=True).astype(jnp.int32)
    counts = lax.optimization_barrier(jnp.sum((flat_cands[:, None] == jnp.arange(GROUPS, dtype=jnp.int32)[None, :]).astype(jnp.int32), axis=0)).astype(jnp.int32)
    starts = (jnp.cumsum(counts) - counts).astype(jnp.int32)
    pad_rows = N_DP * CAP
    padded = jnp.concatenate([sorted_pairs, jnp.zeros((pad_rows,), jnp.int32)])

    def visit_group(group, all_scores):
        pair_ids = lax.dynamic_slice(padded, (starts[group].astype(jnp.int32),), (pad_rows,))
        is_live = jnp.arange(pad_rows, dtype=jnp.int32) < counts[group]
        group_queries = lax.dynamic_index_in_dim(queries, group, 0, keepdims=False)
        group_scores = jnp.dot(unit_grads[pair_ids // CANDS], group_queries.T, preferred_element_type=jnp.float32)
        target = jnp.where(is_live, pair_ids, pair_count).astype(jnp.int32)
        return all_scores.at[target].set(group_scores, mode='drop')
    all_scores = lax.fori_loop(0, GROUPS, visit_group, jnp.zeros((pair_count, QN), jnp.float32))
    return all_scores.reshape(EXAMPLES, CANDS, QN)
```

```python
import functools

import jax
import jax.numpy as jnp
from jax import lax
from jax.experimental import pallas as pl
from jax.experimental.pallas import tpu as pltpu
from jax.sharding import PartitionSpec as P

epsilon = 1e-06
LANES = 128
NT = (((1,), (1,)), ((), ()))
TN = (((0,), (0,)), ((), ()))


def project_kernel(
    groups, ways, steps, cand_ref, act_ref, grad_ref, win_ref, wout_ref,
    keep_ref, far_ref, near_ref, total, wout, rank, start,
):
    step = pl.program_id(0)
    rows = act_ref.shape[0]
    proj_rank = win_ref.shape[0]
    examples = cand_ref.shape[0]
    per_step = examples // steps
    tokens = rows // per_step
    me = lax.axis_index("tensor")

    @pl.when(step == 0)
    def _():
        half = proj_rank // 2
        r = lax.broadcasted_iota(jnp.int32, (proj_rank, proj_rank), 0)
        c = lax.broadcasted_iota(jnp.int32, (proj_rank, proj_rank), 1)
        source = jnp.where(r < half, 2 * r, 2 * (r - half) + 1)
        pick = (c == source).astype(jnp.bfloat16)
        wout[...] = jnp.dot(pick, wout_ref[...], preferred_element_type=jnp.float32).astype(
            jnp.bfloat16
        )
        for g in range(groups + 1):
            start[g] = 0
        for e in range(examples):
            g = cand_ref[e]
            seen = start[g]
            rank[e] = seen
            start[g] = seen + 1
        below = jnp.int32(0)
        for g in range(groups):
            here = start[g]
            start[g] = below
            below = below + here

    act = lax.dot_general(act_ref[...], win_ref[...], NT, preferred_element_type=jnp.float32)
    grad = lax.dot_general(grad_ref[...], wout[...], NT, preferred_element_type=jnp.float32)
    both = jnp.concatenate([grad, act], axis=1)
    share = examples // ways
    for k in range(per_step):
        e = step * per_step + k
        place = start[cand_ref[e]] + rank[e]
        rel = lax.rem(place, ways) ^ me
        part = ((rel & 1) << 1) | (rel >> 1)
        row = (part * share + lax.div(place, ways)) * tokens
        total[pl.ds(pl.multiple_of(row, 8), tokens), :] = both[k * tokens : (k + 1) * tokens]

    @pl.when(step == steps - 1)
    def _():
        size = share * tokens
        keep_ref[...] = total[0 : 2 * size, :]
        near_ref[...] = total[2 * size : 3 * size, :]
        far_ref[...] = total[3 * size : 4 * size, :]


def project(cands, act, grad, win, wout, groups, ways):
    examples = cands.shape[0]
    rows = act.shape[0]
    steps = 8
    block = rows // steps
    share = rows // ways
    f32 = jnp.float32
    whole = lambda shape: pl.BlockSpec(shape, lambda i: (0, 0))
    return pl.pallas_call(
        functools.partial(project_kernel, groups, ways, steps),
        grid=(steps,),
        in_specs=[
            pl.BlockSpec(memory_space=pltpu.SMEM),
            pl.BlockSpec((block, act.shape[1]), lambda i: (i, 0)),
            pl.BlockSpec((block, grad.shape[1]), lambda i: (i, 0)),
            whole(win.shape),
            whole(wout.shape),
        ],
        out_specs=[whole((2 * share, LANES)), whole((share, LANES)), whole((share, LANES))],
        out_shape=[
            jax.ShapeDtypeStruct((2 * share, LANES), f32),
            jax.ShapeDtypeStruct((share, LANES), f32),
            jax.ShapeDtypeStruct((share, LANES), f32),
        ],
        scratch_shapes=[
            pltpu.VMEM((rows, LANES), f32),
            pltpu.VMEM(wout.shape, jnp.bfloat16),
            pltpu.SMEM((examples,), jnp.int32),
            pltpu.SMEM((groups + 1,), jnp.int32),
        ],
        compiler_params=pltpu.CompilerParams(vmem_limit_bytes=32 << 20),
        cost_estimate=pl.CostEstimate(
            flops=2 * rows * (act.shape[1] + grad.shape[1]) * 64,
            bytes_accessed=2 * rows * (act.shape[1] + grad.shape[1]),
            transcendentals=0,
        ),
        name="project",
    )(cands, act, grad, win, wout)


def unit_kernel(tokens, chunks, row_ref, a_ref, b_ref, c_ref, out_ref, total):
    total[...] = a_ref[...] + b_ref[...] + c_ref[...]
    out_ref[...] = jnp.zeros_like(out_ref)
    count = total.shape[0] // tokens
    half = LANES // 2
    width = chunks * LANES
    low = lax.broadcasted_iota(jnp.int32, (chunks, LANES), 1) < half
    low_t = lax.broadcasted_iota(jnp.int32, (tokens, LANES), 1) < half
    for i in range(count):
        part = total[i * tokens : (i + 1) * tokens, :]
        twice = jnp.where(low_t, pltpu.roll(part, half, 1), part)
        g_hi = part.astype(jnp.bfloat16).astype(jnp.float32)
        a_hi = twice.astype(jnp.bfloat16).astype(jnp.float32)
        left = jnp.concatenate([g_hi, g_hi, part - g_hi], axis=0)[:, :half].astype(jnp.bfloat16)
        right = jnp.concatenate([a_hi, twice - a_hi, a_hi], axis=0).astype(jnp.bfloat16)
        prod = lax.dot_general(left, right, TN, preferred_element_type=jnp.float32)
        entries = jnp.where(low, prod[:chunks], prod[chunks : 2 * chunks])
        square = jnp.sum(entries * entries, axis=0, keepdims=True)
        mean = jnp.sum(square, axis=1, keepdims=True) / width
        unit = (entries * lax.rsqrt(mean + epsilon)).astype(jnp.bfloat16)
        row = pl.multiple_of(row_ref[i] * chunks, chunks)
        out_ref[pl.ds(row, chunks), :] = unit


def unit_grads(slots, a, b, c, tokens, chunks, slot_count):
    whole = pl.BlockSpec(memory_space=pltpu.VMEM)
    return pl.pallas_call(
        functools.partial(unit_kernel, tokens, chunks),
        in_specs=[pl.BlockSpec(memory_space=pltpu.SMEM), whole, whole, whole],
        out_specs=whole,
        out_shape=jax.ShapeDtypeStruct((slot_count * chunks, LANES), jnp.bfloat16),
        scratch_shapes=[pltpu.VMEM(a.shape, jnp.float32)],
        cost_estimate=pl.CostEstimate(flops=20_000_000, bytes_accessed=1_000_000, transcendentals=0),
        name="unit_grads",
    )(slots, a, b, c)


def score_kernel(
    groups, slots, padded, first, chunks, parts, has_prev, x0_ref, x1_ref, q_ref, *rest
):
    prev_ref = rest[0] if has_prev else None
    out_ref, stage, units, queries, sems = rest[has_prev:]
    width = chunks // parts * LANES
    copies = [
        pltpu.make_async_copy(
            q_ref.at[:, pl.ds(k * width, width)], queries.at[k], sems.at[k]
        )
        for k in range(parts)
    ]
    for copy in copies:
        copy.start()
    span = slots * chunks
    for d in range(groups):
        base = d * padded * chunks
        if first:
            stage[base : base + first * chunks, :] = jnp.zeros((first * chunks, LANES), jnp.float32)
        for n, x_ref in enumerate((x0_ref, x1_ref)):
            at = base + (first + n * slots) * chunks
            stage[at : at + span, :] = x_ref[d * span : (d + 1) * span, :].astype(jnp.float32)
        at = base + (first + 2 * slots) * chunks
        left = (padded - first - 2 * slots) * chunks
        stage[at : at + left, :] = jnp.zeros((left, LANES), jnp.float32)
    rows = groups * padded
    total = prev_ref[...] if has_prev else None
    for k in range(parts):
        for j in range(chunks // parts):
            piece = stage[pl.ds(k * (chunks // parts) + j, rows, stride=chunks), :]
            units[:, j * LANES : (j + 1) * LANES] = piece.astype(jnp.bfloat16)
        copies[k].wait()
        add = lax.dot_general(units[...], queries[k], NT, preferred_element_type=jnp.float32)
        total = add if total is None else total + add
    out_ref[...] = total.astype(out_ref.dtype)


def scores_of(x0, x1, queries, prev, groups, slots, padded, first, out_dtype):
    chunks = queries.shape[1] // LANES
    parts = 4
    rows = groups * padded
    vmem = pl.BlockSpec(memory_space=pltpu.VMEM)
    operands = [x0, x1, queries] + ([prev] if prev is not None else [])
    specs = [vmem, vmem, pl.BlockSpec(memory_space=pl.ANY)] + ([vmem] if prev is not None else [])
    width = queries.shape[1] // parts
    return pl.pallas_call(
        functools.partial(
            score_kernel, groups, slots, padded, first, chunks, parts, int(prev is not None)
        ),
        in_specs=specs,
        out_specs=vmem,
        out_shape=jax.ShapeDtypeStruct((rows, queries.shape[0]), out_dtype),
        scratch_shapes=[
            pltpu.VMEM((rows * chunks, LANES), jnp.float32),
            pltpu.VMEM((rows, width), jnp.bfloat16),
            pltpu.VMEM((parts, queries.shape[0], width), jnp.bfloat16),
            pltpu.SemaphoreType.DMA((parts,)),
        ],
        compiler_params=pltpu.CompilerParams(vmem_limit_bytes=32 << 20),
        cost_estimate=pl.CostEstimate(
            flops=2 * rows * queries.shape[0] * queries.shape[1],
            bytes_accessed=2 * queries.size,
            transcendentals=0,
        ),
        name="scores",
    )(*operands)


def pick_kernel(row_ref, x_ref, out_ref):
    count = row_ref.shape[0]
    rows = x_ref.shape[0]
    parts = x_ref.shape[1] // LANES
    hit = lax.broadcasted_iota(jnp.int32, (count, rows), 1) == row_ref[...]
    pick = jnp.where(hit, 1.0, 0.0).astype(jnp.bfloat16)
    got = jnp.dot(pick, x_ref[...], preferred_element_type=jnp.float32)
    for j in range(parts):
        out_ref[pl.ds(j, count, stride=parts), :] = got[:, j * LANES : (j + 1) * LANES]


def pick_rows(row, x):
    vmem = pl.BlockSpec(memory_space=pltpu.VMEM)
    count, width = row.shape[0], x.shape[1]
    return pl.pallas_call(
        pick_kernel,
        in_specs=[vmem, vmem],
        out_specs=vmem,
        out_shape=jax.ShapeDtypeStruct((count * (width // LANES), LANES), jnp.float32),
        cost_estimate=pl.CostEstimate(flops=16_000_000, bytes_accessed=400_000, transcendentals=0),
        name="pick_rows",
    )(row, x)


def local_one(activations, out_grads, proj_in, proj_out, queries, candidates):
    examples, tokens, hidden = activations.shape
    features = out_grads.shape[2]
    groups = lax.axis_size("dp")
    ways = lax.axis_size("tensor")
    me = lax.axis_index("tensor")
    capacity = max(2, 5 * examples // (2 * groups))
    slots = -(-capacity // ways)
    padded = -(-ways * slots // 8) * 8
    query_block = queries[0]
    chunks = query_block.shape[1] // LANES
    core = [(i, i ^ 1) for i in range(ways)]
    across = [(i, i ^ 2) for i in range(ways)]

    cands = candidates.reshape(-1)
    keep, far, near = project(
        cands,
        activations.reshape(examples * tokens, hidden),
        out_grads.reshape(examples * tokens, features),
        proj_in.T,
        proj_out.T,
        groups,
        ways,
    )
    share = far.shape[0]
    far_in = lax.ppermute(far, "tensor", core)
    near_in = lax.ppermute(near, "tensor", core)
    across_in = lax.ppermute(keep[share:] + far_in, "tensor", across)

    number = jnp.arange(examples, dtype=jnp.int32)
    before = (cands[None, :] < cands[:, None]) | (
        (cands[None, :] == cands[:, None]) & (number[None, :] < number[:, None])
    )
    place = jnp.sum(before.astype(jnp.int32), axis=1)
    start = jnp.sum((cands[None, :] < cands[:, None]).astype(jnp.int32), axis=1)
    owner = place % ways
    slot = place // ways - (start + ways - 1 - owner) // ways
    mine = (
        place[None, :] == ways * jnp.arange(examples // ways, dtype=jnp.int32)[:, None] + me
    )
    my_slots = jnp.sum(jnp.where(mine, (cands * slots + slot)[None, :], 0), axis=1)
    pick = (cands * padded + (owner ^ me) * slots + slot)[:, None]

    units = unit_grads(my_slots, keep[:share], near_in, across_in, tokens, chunks, groups * slots)
    shape = (groups, slots * chunks, LANES)
    own = lax.all_to_all(units.reshape(shape), "dp", split_axis=0, concat_axis=0, tiled=True)
    own = own.reshape(units.shape)
    over_y = lax.ppermute(own, "tensor", across)
    over_core = lax.ppermute(own, "tensor", core)
    over_both = lax.ppermute(over_y, "tensor", core)
    first = scores_of(
        own, over_core, query_block, None, groups, slots, padded, 0, jnp.float32
    )
    both = scores_of(
        over_y, over_both, query_block, first, groups, slots, padded, 2 * slots, jnp.bfloat16
    )
    block = both.reshape(groups, padded, both.shape[1])
    returned = lax.all_to_all(block, "dp", split_axis=0, concat_axis=0, tiled=True)
    picked = pick_rows(pick, returned.reshape(both.shape))
    return picked.reshape(examples, 1, both.shape[1])


def local_many(activations, out_grads, proj_in, proj_out, queries, candidates):
    examples_here, tokens_here, hidden_here = activations.shape
    proj_rank = proj_in.shape[1]
    per_example = candidates.shape[1]
    groups = lax.axis_size("dp")
    capacity = max(2, 5 * examples_here * per_example // (2 * groups))
    act_proj = jnp.dot(
        activations.reshape(examples_here * tokens_here, hidden_here),
        proj_in,
        preferred_element_type=jnp.float32,
    )
    grad_proj = jnp.dot(
        out_grads.reshape(examples_here * tokens_here, out_grads.shape[2]),
        proj_out,
        preferred_element_type=jnp.float32,
    )
    both_proj = jnp.concatenate([grad_proj, act_proj], axis=1).reshape(
        examples_here, tokens_here, 2 * proj_rank
    )
    summed = lax.psum(both_proj, "tensor")
    grad_side = summed[:, :, :proj_rank]
    act_side = summed[:, :, proj_rank:]
    example_grads = jnp.einsum(
        "eta,etb->eab", grad_side, act_side, precision=lax.Precision.HIGHEST
    ).reshape(examples_here, proj_rank * proj_rank)
    inv_rms = lax.rsqrt(jnp.mean(example_grads * example_grads, axis=1, keepdims=True) + epsilon)
    unit = (example_grads * inv_rms).astype(jnp.bfloat16)
    flat_cands = candidates.reshape(-1)
    hit_table = (flat_cands[:, None] == jnp.arange(groups, dtype=jnp.int32)[None, :]).astype(
        jnp.int32
    )
    earlier = jnp.cumsum(hit_table, axis=0) - hit_table
    slot_index = jnp.sum(earlier * hit_table, axis=1)
    dest_index = flat_cands * capacity + slot_index
    row_copies = jnp.repeat(unit, per_example, axis=0)
    grad_width = unit.shape[1]
    send_buffer = (
        jnp.zeros((groups * capacity, grad_width), jnp.bfloat16).at[dest_index].set(row_copies)
    )
    send_buffer = send_buffer.reshape(groups, capacity, grad_width)
    col_width = grad_width // lax.axis_size("tensor")
    column_part = lax.dynamic_slice_in_dim(
        send_buffer, lax.axis_index("tensor") * col_width, col_width, 2
    )
    received = lax.all_to_all(column_part, "dp", split_axis=0, concat_axis=0, tiled=True)
    slot_scores = jnp.einsum(
        "gsk,qk->gsq",
        lax.all_gather(received, "tensor", axis=2, tiled=True),
        queries[0],
        preferred_element_type=jnp.float32,
    )
    returned = lax.all_to_all(slot_scores, "dp", split_axis=0, concat_axis=0, tiled=True)
    picked = returned.reshape(groups * capacity, returned.shape[2])[dest_index]
    return picked.reshape(examples_here, per_example, returned.shape[2])


def local(activations, out_grads, proj_in, proj_out, queries, candidates):
    one = candidates.shape[1] == 1 and lax.axis_size("tensor") == 4
    return (local_one if one else local_many)(
        activations, out_grads, proj_in, proj_out, queries, candidates
    )


def solution(mesh):
    placed = (
        P("dp", None, "tensor"),
        P("dp", None, "tensor"),
        P("tensor", None),
        P("tensor", None),
        P("dp", "tensor", None),
        P("dp", None),
    )
    return jax.shard_map(
        local, mesh=mesh, in_specs=placed, out_specs=P("dp", None, "tensor"), check_vma=False
    )
```

```python
import functools

import jax
import jax.numpy as jnp
from jax import lax
from jax.experimental import pallas as pl
from jax.experimental.pallas import tpu as pltpu
from jax.sharding import PartitionSpec as P

epsilon = 1e-06
LANES = 128
NT = (((1,), (1,)), ((), ()))
TN = (((0,), (0,)), ((), ()))


def project_kernel(
    groups, ways, tokens, blocks, cand_hbm, act_hbm, grad_hbm, win_hbm, wout_hbm,
    own_ref, over_ref, near_ref, far_ref,
    act, grad, win, wout, raw, dealt, cand, rank, start, act_sems, grad_sems, sems,
):
    proj_rank = win.shape[0]
    examples = cand.shape[1]
    share = examples // ways
    step = act.shape[0] // act_sems.shape[0]
    me = lax.axis_index("tensor")

    def piece(i):
        return pl.ds(pl.multiple_of(i * step, step), step)

    def act_copy(i):
        return pltpu.make_async_copy(act_hbm.at[piece(i)], act.at[piece(i)], act_sems.at[i])

    def grad_copy(i):
        return pltpu.make_async_copy(grad_hbm.at[piece(i)], grad.at[piece(i)], grad_sems.at[i])

    cand_copy = pltpu.make_async_copy(cand_hbm, cand, sems.at[0])
    raw_copy = pltpu.make_async_copy(wout_hbm, raw, sems.at[1])
    win_copy = pltpu.make_async_copy(win_hbm, win, sems.at[2])
    cand_copy.start()
    raw_copy.start()
    win_copy.start()

    @pl.loop(0, act_sems.shape[0])
    def _(i):
        act_copy(i).start()
        grad_copy(i).start()

    cand_copy.wait()

    @pl.loop(0, groups)
    def _(g):
        start[g] = 0

    @pl.loop(0, examples)
    def _(e):
        g = cand[0, e]
        rank[e] = start[g]
        start[g] = start[g] + 1

    def shift(g, below):
        here = start[g]
        start[g] = below
        return below + here

    lax.fori_loop(0, groups, shift, jnp.int32(0))

    half = proj_rank // 2
    r = lax.broadcasted_iota(jnp.int32, (proj_rank, proj_rank), 0)
    c = lax.broadcasted_iota(jnp.int32, (proj_rank, proj_rank), 1)
    pick = (c == jnp.where(r < half, 2 * r, 2 * (r - half) + 1)).astype(jnp.bfloat16)
    raw_copy.wait()
    wout[...] = jnp.dot(pick, raw[...], preferred_element_type=jnp.float32).astype(jnp.bfloat16)
    win_copy.wait()

    done = 0
    for count, rows in blocks:

        @pl.loop(0, count)
        def _(i, done=done, rows=rows):
            for j in range(rows // step):
                act_copy(done // step + i * (rows // step) + j).wait()
                grad_copy(done // step + i * (rows // step) + j).wait()
            at = pl.multiple_of(done + i * rows, step)
            here = pl.ds(at, rows)
            left = lax.dot_general(grad[here, :], wout[...], NT, preferred_element_type=jnp.float32)
            right = lax.dot_general(act[here, :], win[...], NT, preferred_element_type=jnp.float32)
            both = jnp.concatenate([left, right], axis=1)
            first = done // tokens + i * (rows // tokens)
            for k in range(rows // tokens):
                e = first + k
                place = start[cand[0, e]] + rank[e]
                part = (place & (ways - 1)) ^ me
                row = (part * share + place // ways) * tokens
                dealt[pl.ds(pl.multiple_of(row, 8), tokens), :] = both[
                    k * tokens : (k + 1) * tokens
                ]

        done += count * rows

    size = share * tokens
    for r, ref in enumerate((own_ref, near_ref, over_ref, far_ref)):
        ref[...] = dealt[r * size : (r + 1) * size, :]


def project(cands, act, grad, win, wout, tokens, groups, ways):
    examples = cands.shape[1]
    rows = act.shape[0]
    pieces = 8
    step = rows // pieces
    blocks = ((3, 2 * step), (2, step))
    share = rows // ways
    hbm = pl.BlockSpec(memory_space=pltpu.HBM)
    vmem = pl.BlockSpec(memory_space=pltpu.VMEM)
    return pl.pallas_call(
        functools.partial(project_kernel, groups, ways, tokens, blocks),
        in_specs=[hbm] * 5,
        out_specs=[vmem] * 4,
        out_shape=[jax.ShapeDtypeStruct((share, LANES), jnp.float32)] * 4,
        scratch_shapes=[
            pltpu.VMEM(act.shape, jnp.bfloat16),
            pltpu.VMEM(grad.shape, jnp.bfloat16),
            pltpu.VMEM(win.shape, jnp.bfloat16),
            pltpu.VMEM(wout.shape, jnp.bfloat16),
            pltpu.VMEM(wout.shape, jnp.bfloat16),
            pltpu.VMEM((rows, LANES), jnp.float32),
            pltpu.SMEM((1, examples), jnp.int32),
            pltpu.SMEM((examples,), jnp.int32),
            pltpu.SMEM((groups,), jnp.int32),
            pltpu.SemaphoreType.DMA((pieces,)),
            pltpu.SemaphoreType.DMA((pieces,)),
            pltpu.SemaphoreType.DMA((3,)),
        ],
        compiler_params=pltpu.CompilerParams(vmem_limit_bytes=61 << 20),
        cost_estimate=pl.CostEstimate(
            flops=2 * rows * (act.shape[1] + grad.shape[1]) * 64,
            bytes_accessed=2 * rows * (act.shape[1] + grad.shape[1]),
            transcendentals=0,
        ),
        name="project",
    )(cands, act, grad, win, wout)


def unit_kernel(tokens, chunks, row_ref, a_ref, b_ref, out_ref, total):
    total[...] = a_ref[...] + b_ref[...]
    out_ref[...] = jnp.zeros_like(out_ref)
    count = total.shape[0] // tokens
    half = LANES // 2
    width = chunks * LANES
    low = lax.broadcasted_iota(jnp.int32, (chunks, LANES), 1) < half
    low_t = lax.broadcasted_iota(jnp.int32, (tokens, LANES), 1) < half

    @pl.loop(0, count, unroll=4)
    def _(i):
        part = total[pl.ds(pl.multiple_of(i * tokens, 8), tokens), :]
        twice = jnp.where(low_t, pltpu.roll(part, half, 1), part)
        g_hi = part.astype(jnp.bfloat16).astype(jnp.float32)
        a_hi = twice.astype(jnp.bfloat16).astype(jnp.float32)
        left = jnp.concatenate([g_hi, g_hi, part - g_hi], axis=0)[:, :half].astype(jnp.bfloat16)
        right = jnp.concatenate([a_hi, twice - a_hi, a_hi], axis=0).astype(jnp.bfloat16)
        prod = lax.dot_general(left, right, TN, preferred_element_type=jnp.float32)
        entries = jnp.where(low, prod[:chunks], prod[chunks : 2 * chunks])
        square = jnp.sum(entries * entries, axis=0, keepdims=True)
        mean = jnp.sum(square, axis=1, keepdims=True) / width
        unit = (entries * lax.rsqrt(mean + epsilon)).astype(jnp.bfloat16)
        row = pl.multiple_of(row_ref[i] * chunks, chunks)
        out_ref[pl.ds(row, chunks), :] = unit


def unit_grads(slots, a, b, tokens, chunks, slot_count):
    whole = pl.BlockSpec(memory_space=pltpu.VMEM)
    return pl.pallas_call(
        functools.partial(unit_kernel, tokens, chunks),
        in_specs=[pl.BlockSpec(memory_space=pltpu.SMEM), whole, whole],
        out_specs=whole,
        out_shape=jax.ShapeDtypeStruct((slot_count * chunks, LANES), jnp.bfloat16),
        scratch_shapes=[pltpu.VMEM(a.shape, jnp.float32)],
        compiler_params=pltpu.CompilerParams(vmem_limit_bytes=16 << 20),
        cost_estimate=pl.CostEstimate(flops=20_000_000, bytes_accessed=1_000_000, transcendentals=0),
        name="unit_grads",
    )(slots, a, b)


def score_kernel(groups, slots, padded, first, chunks, parts, x0_ref, x1_ref, q_hbm, *rest):
    prev_ref = rest[0] if first else None
    out_ref, stage, units, queries, total, sems = rest[1 if first else 0 :]
    each = chunks // parts
    width = each * LANES
    span = slots * chunks
    after = padded - first - 2 * slots

    def load(k):
        columns = pl.ds(pl.multiple_of(k * width, width), width)
        return pltpu.make_async_copy(q_hbm.at[:, columns], queries.at[k], sems.at[k])

    for k in range(parts):
        load(k).start()

    @pl.loop(0, groups)
    def _(d):
        base = d * padded * each
        for k in range(parts):
            if first:
                stage[k, pl.ds(base, first * each), :] = jnp.zeros(
                    (first * each, LANES), jnp.float32
                )
            stage[k, pl.ds(base + (first + 2 * slots) * each, after * each), :] = jnp.zeros(
                (after * each, LANES), jnp.float32
            )
        for n, x_ref in enumerate((x0_ref, x1_ref)):
            got = x_ref[pl.ds(pl.multiple_of(d * span, span), span), :].astype(jnp.float32)
            got = got.reshape(slots, parts, each, LANES)
            for k in range(parts):
                at = pl.ds(base + (first + n * slots) * each, slots * each)
                stage[k, at, :] = got[:, k].reshape(slots * each, LANES)

    rows = groups * padded
    total[...] = jnp.zeros_like(total)

    @pl.loop(0, parts)
    def _(k):
        for j in range(each):
            piece = stage[k, pl.ds(j, rows, stride=each), :]
            units[:, j * LANES : (j + 1) * LANES] = piece.astype(jnp.bfloat16)
        load(k).wait()
        total[...] += lax.dot_general(
            queries[k], units[...], NT, preferred_element_type=jnp.float32
        )

    out = total[...].T
    if first:
        out = out + prev_ref[...]
    out_ref[...] = out.astype(out_ref.dtype)


def scores_of(x0, x1, queries, prev, groups, slots, padded, first):
    parts = 4
    count, width = queries.shape[0], queries.shape[1] // parts
    chunks = queries.shape[1] // LANES
    rows = groups * padded
    vmem = pl.BlockSpec(memory_space=pltpu.VMEM)
    return pl.pallas_call(
        functools.partial(score_kernel, groups, slots, padded, first, chunks, parts),
        in_specs=[vmem, vmem, pl.BlockSpec(memory_space=pltpu.HBM)] + ([vmem] if first else []),
        out_specs=vmem,
        out_shape=jax.ShapeDtypeStruct((rows, count), jnp.bfloat16 if first else jnp.float32),
        scratch_shapes=[
            pltpu.VMEM((parts, rows * (chunks // parts), LANES), jnp.float32),
            pltpu.VMEM((rows, width), jnp.bfloat16),
            pltpu.VMEM((parts, count, width), jnp.bfloat16),
            pltpu.VMEM((count, rows), jnp.float32),
            pltpu.SemaphoreType.DMA((parts,)),
        ],
        compiler_params=pltpu.CompilerParams(vmem_limit_bytes=50 << 20),
        cost_estimate=pl.CostEstimate(
            flops=2 * rows * queries.size, bytes_accessed=2 * queries.size, transcendentals=0
        ),
        name="scores",
    )(x0, x1, queries, *([prev] if first else []))


def pick_kernel(row_ref, x_ref, out_ref):
    count = row_ref.shape[0]
    rows = x_ref.shape[0]
    parts = x_ref.shape[1] // LANES
    hit = lax.broadcasted_iota(jnp.int32, (count, rows), 1) == row_ref[...]
    pick = jnp.where(hit, 1.0, 0.0).astype(jnp.bfloat16)
    got = jnp.dot(pick, x_ref[...], preferred_element_type=jnp.float32)
    for j in range(parts):
        out_ref[pl.ds(j, count, stride=parts), :] = got[:, j * LANES : (j + 1) * LANES]


def pick_rows(row, x):
    vmem = pl.BlockSpec(memory_space=pltpu.VMEM)
    count, width = row.shape[0], x.shape[1]
    return pl.pallas_call(
        pick_kernel,
        in_specs=[vmem, vmem],
        out_specs=vmem,
        out_shape=jax.ShapeDtypeStruct((count * (width // LANES), LANES), jnp.float32),
        compiler_params=pltpu.CompilerParams(vmem_limit_bytes=16 << 20),
        cost_estimate=pl.CostEstimate(flops=16_000_000, bytes_accessed=400_000, transcendentals=0),
        name="pick_rows",
    )(row, x)


def local_one(activations, out_grads, proj_in, proj_out, queries, candidates):
    examples, tokens, hidden = activations.shape
    features = out_grads.shape[2]
    groups = lax.axis_size("dp")
    ways = lax.axis_size("tensor")
    me = lax.axis_index("tensor")
    capacity = max(2, 5 * examples // (2 * groups))
    slots = -(-capacity // ways)
    padded = -(-ways * slots // 8) * 8
    query_block = queries[0]
    chunks = query_block.shape[1] // LANES
    core = [(i, i ^ 1) for i in range(ways)]
    across = [(i, i ^ 2) for i in range(ways)]

    cands = candidates.reshape(-1)
    own_part, over_part, near_part, far_part = project(
        candidates.reshape(1, examples),
        activations.reshape(examples * tokens, hidden),
        out_grads.reshape(examples * tokens, features),
        proj_in.T,
        proj_out.T,
        tokens,
        groups,
        ways,
    )
    far_in = lax.ppermute(far_part, "tensor", core)
    near_in = lax.ppermute(near_part, "tensor", core)
    across_in = lax.ppermute(over_part + far_in, "tensor", across)

    number = jnp.arange(examples, dtype=jnp.int32)
    before = (cands[None, :] < cands[:, None]) | (
        (cands[None, :] == cands[:, None]) & (number[None, :] < number[:, None])
    )
    place = jnp.sum(before.astype(jnp.int32), axis=1)
    start = jnp.sum((cands[None, :] < cands[:, None]).astype(jnp.int32), axis=1)
    owner = place % ways
    slot = place // ways - (start + ways - 1 - owner) // ways
    mine = (
        place[None, :] == ways * jnp.arange(examples // ways, dtype=jnp.int32)[:, None] + me
    )
    my_slots = jnp.sum(jnp.where(mine, (cands * slots + slot)[None, :], 0), axis=1)
    pick = (cands * padded + (owner ^ me) * slots + slot)[:, None]

    units = unit_grads(my_slots, own_part + near_in, across_in, tokens, chunks, groups * slots)
    shape = (groups, slots * chunks, LANES)
    own = lax.all_to_all(units.reshape(shape), "dp", split_axis=0, concat_axis=0, tiled=True)
    own = own.reshape(units.shape)
    over_y = lax.ppermute(own, "tensor", across)
    over_core = lax.ppermute(own, "tensor", core)
    first = scores_of(own, over_core, query_block, None, groups, slots, padded, 0)
    over_y, first = lax.optimization_barrier((over_y, first))
    over_both = lax.ppermute(over_y, "tensor", core)
    both = scores_of(over_y, over_both, query_block, first, groups, slots, padded, 2 * slots)
    block = both.reshape(groups, padded, both.shape[1])
    returned = lax.all_to_all(block, "dp", split_axis=0, concat_axis=0, tiled=True)
    picked = pick_rows(pick, returned.reshape(both.shape))
    return picked.reshape(examples, 1, both.shape[1])


def local_many(activations, out_grads, proj_in, proj_out, queries, candidates):
    examples_here, tokens_here, hidden_here = activations.shape
    proj_rank = proj_in.shape[1]
    per_example = candidates.shape[1]
    groups = lax.axis_size("dp")
    capacity = max(2, 5 * examples_here * per_example // (2 * groups))
    act_proj = jnp.dot(
        activations.reshape(examples_here * tokens_here, hidden_here),
        proj_in,
        preferred_element_type=jnp.float32,
    )
    grad_proj = jnp.dot(
        out_grads.reshape(examples_here * tokens_here, out_grads.shape[2]),
        proj_out,
        preferred_element_type=jnp.float32,
    )
    both_proj = jnp.concatenate([grad_proj, act_proj], axis=1).reshape(
        examples_here, tokens_here, 2 * proj_rank
    )
    summed = lax.psum(both_proj, "tensor")
    grad_side = summed[:, :, :proj_rank]
    act_side = summed[:, :, proj_rank:]
    example_grads = jnp.einsum(
        "eta,etb->eab", grad_side, act_side, precision=lax.Precision.HIGHEST
    ).reshape(examples_here, proj_rank * proj_rank)
    inv_rms = lax.rsqrt(jnp.mean(example_grads * example_grads, axis=1, keepdims=True) + epsilon)
    unit = (example_grads * inv_rms).astype(jnp.bfloat16)
    flat_cands = candidates.reshape(-1)
    hit_table = (flat_cands[:, None] == jnp.arange(groups, dtype=jnp.int32)[None, :]).astype(
        jnp.int32
    )
    earlier = jnp.cumsum(hit_table, axis=0) - hit_table
    slot_index = jnp.sum(earlier * hit_table, axis=1)
    dest_index = flat_cands * capacity + slot_index
    row_copies = jnp.repeat(unit, per_example, axis=0)
    grad_width = unit.shape[1]
    send_buffer = (
        jnp.zeros((groups * capacity, grad_width), jnp.bfloat16).at[dest_index].set(row_copies)
    )
    send_buffer = send_buffer.reshape(groups, capacity, grad_width)
    col_width = grad_width // lax.axis_size("tensor")
    column_part = lax.dynamic_slice_in_dim(
        send_buffer, lax.axis_index("tensor") * col_width, col_width, 2
    )
    received = lax.all_to_all(column_part, "dp", split_axis=0, concat_axis=0, tiled=True)
    slot_scores = jnp.einsum(
        "gsk,qk->gsq",
        lax.all_gather(received, "tensor", axis=2, tiled=True),
        queries[0],
        preferred_element_type=jnp.float32,
    )
    returned = lax.all_to_all(slot_scores, "dp", split_axis=0, concat_axis=0, tiled=True)
    picked = returned.reshape(groups * capacity, returned.shape[2])[dest_index]
    return picked.reshape(examples_here, per_example, returned.shape[2])


def local(activations, out_grads, proj_in, proj_out, queries, candidates):
    one = candidates.shape[1] == 1 and lax.axis_size("tensor") == 4
    return (local_one if one else local_many)(
        activations, out_grads, proj_in, proj_out, queries, candidates
    )


def solution(mesh):
    placed = (
        P("dp", None, "tensor"),
        P("dp", None, "tensor"),
        P("tensor", None),
        P("tensor", None),
        P("dp", "tensor", None),
        P("dp", None),
    )
    return jax.shard_map(
        local, mesh=mesh, in_specs=placed, out_specs=P("dp", None, "tensor"), check_vma=False
    )
```

```python
import functools

import jax
import jax.numpy as jnp
from jax import lax
from jax.experimental import pallas as pl
from jax.experimental.pallas import tpu as pltpu
from jax.sharding import PartitionSpec as P

epsilon = 1e-06
LANES = 128
NT = (((1,), (1,)), ((), ()))
TN = (((0,), (0,)), ((), ()))


def project_kernel(
    groups, ways, tokens, slots, padded, blocks,
    cand_hbm, act_hbm, grad_hbm, win_hbm, wout_hbm,
    own_ref, over_ref, near_ref, far_ref, slot_ref, pick_ref,
    act, grad, win, wout, raw, dealt, cand, rank, start, act_sems, grad_sems, sems,
):
    proj_rank = win.shape[0]
    examples = cand.shape[1]
    share = examples // ways
    step = act.shape[0] // act_sems.shape[0]
    me = lax.axis_index("tensor")

    def piece(i):
        return pl.ds(pl.multiple_of(i * step, step), step)

    def act_copy(i):
        return pltpu.make_async_copy(act_hbm.at[piece(i)], act.at[piece(i)], act_sems.at[i])

    def grad_copy(i):
        return pltpu.make_async_copy(grad_hbm.at[piece(i)], grad.at[piece(i)], grad_sems.at[i])

    cand_copy = pltpu.make_async_copy(cand_hbm, cand, sems.at[0])
    raw_copy = pltpu.make_async_copy(wout_hbm, raw, sems.at[1])
    win_copy = pltpu.make_async_copy(win_hbm, win, sems.at[2])
    cand_copy.start()
    raw_copy.start()
    win_copy.start()

    @pl.loop(0, act_sems.shape[0])
    def _(i):
        act_copy(i).start()
        grad_copy(i).start()

    cand_copy.wait()

    @pl.loop(0, groups)
    def _(g):
        start[g] = 0

    @pl.loop(0, examples)
    def _(e):
        g = cand[0, e]
        rank[e] = start[g]
        start[g] = start[g] + 1

    def shift(g, below):
        here = start[g]
        start[g] = below
        return below + here

    lax.fori_loop(0, groups, shift, jnp.int32(0))

    half = proj_rank // 2
    r = lax.broadcasted_iota(jnp.int32, (proj_rank, proj_rank), 0)
    c = lax.broadcasted_iota(jnp.int32, (proj_rank, proj_rank), 1)
    pick = (c == jnp.where(r < half, 2 * r, 2 * (r - half) + 1)).astype(jnp.bfloat16)
    raw_copy.wait()
    wout[...] = jnp.dot(pick, raw[...], preferred_element_type=jnp.float32).astype(jnp.bfloat16)
    win_copy.wait()

    done = 0
    for count, rows in blocks:

        @pl.loop(0, count)
        def _(i, done=done, rows=rows):
            for j in range(rows // step):
                act_copy(done // step + i * (rows // step) + j).wait()
                grad_copy(done // step + i * (rows // step) + j).wait()
            at = pl.multiple_of(done + i * rows, step)
            here = pl.ds(at, rows)
            left = lax.dot_general(grad[here, :], wout[...], NT, preferred_element_type=jnp.float32)
            right = lax.dot_general(act[here, :], win[...], NT, preferred_element_type=jnp.float32)
            both = jnp.concatenate([left, right], axis=1)
            first = done // tokens + i * (rows // tokens)
            for k in range(rows // tokens):
                e = first + k
                g = cand[0, e]
                place = start[g] + rank[e]
                owner = place & (ways - 1)
                turn = place >> (ways.bit_length() - 1)
                before = (start[g] + ways - 1 - owner) >> (ways.bit_length() - 1)
                rel = owner ^ me
                slot_ref[rel * share + turn] = g * slots + turn - before
                pick_ref[0, e] = g * padded + rel * slots + turn - before
                row = (rel * share + turn) * tokens
                dealt[pl.ds(pl.multiple_of(row, 8), tokens), :] = both[
                    k * tokens : (k + 1) * tokens
                ]

        done += count * rows

    size = share * tokens
    for r, ref in enumerate((own_ref, near_ref, over_ref, far_ref)):
        ref[...] = dealt[r * size : (r + 1) * size, :]


def project(cands, act, grad, win, wout, tokens, groups, ways, slots, padded):
    examples = cands.shape[1]
    rows = act.shape[0]
    pieces = 8
    step = rows // pieces
    blocks = ((3, 2 * step), (2, step))
    share = rows // ways
    hbm = pl.BlockSpec(memory_space=pltpu.HBM)
    vmem = pl.BlockSpec(memory_space=pltpu.VMEM)
    return pl.pallas_call(
        functools.partial(project_kernel, groups, ways, tokens, slots, padded, blocks),
        in_specs=[hbm] * 5,
        out_specs=[vmem] * 4 + [pl.BlockSpec(memory_space=pltpu.SMEM)] * 2,
        out_shape=[jax.ShapeDtypeStruct((share, LANES), jnp.float32)] * 4
        + [
            jax.ShapeDtypeStruct((examples,), jnp.int32),
            jax.ShapeDtypeStruct((1, examples), jnp.int32),
        ],
        scratch_shapes=[
            pltpu.VMEM(act.shape, jnp.bfloat16),
            pltpu.VMEM(grad.shape, jnp.bfloat16),
            pltpu.VMEM(win.shape, jnp.bfloat16),
            pltpu.VMEM(wout.shape, jnp.bfloat16),
            pltpu.VMEM(wout.shape, jnp.bfloat16),
            pltpu.VMEM((rows, LANES), jnp.float32),
            pltpu.SMEM((1, examples), jnp.int32),
            pltpu.SMEM((examples,), jnp.int32),
            pltpu.SMEM((groups,), jnp.int32),
            pltpu.SemaphoreType.DMA((pieces,)),
            pltpu.SemaphoreType.DMA((pieces,)),
            pltpu.SemaphoreType.DMA((3,)),
        ],
        compiler_params=pltpu.CompilerParams(vmem_limit_bytes=61 << 20),
        cost_estimate=pl.CostEstimate(
            flops=2 * rows * (act.shape[1] + grad.shape[1]) * 64,
            bytes_accessed=2 * rows * (act.shape[1] + grad.shape[1]),
            transcendentals=0,
        ),
        name="project",
    )(cands, act, grad, win, wout)


def own_kernel(slot_ref, a_ref, b_ref, out_slot_ref, out_ref):
    out_ref[...] = a_ref[...] + b_ref[...]

    @pl.loop(0, out_slot_ref.shape[0])
    def _(i):
        out_slot_ref[i] = slot_ref[i]


def own_sum(slots, a, b, count):
    smem = pl.BlockSpec(memory_space=pltpu.SMEM)
    vmem = pl.BlockSpec(memory_space=pltpu.VMEM)
    return pl.pallas_call(
        own_kernel,
        in_specs=[smem, vmem, vmem],
        out_specs=[smem, vmem],
        out_shape=[
            jax.ShapeDtypeStruct((count,), jnp.int32),
            jax.ShapeDtypeStruct(a.shape, a.dtype),
        ],
        compiler_params=pltpu.CompilerParams(vmem_limit_bytes=16 << 20),
        cost_estimate=pl.CostEstimate(flops=a.size, bytes_accessed=12 * a.size, transcendentals=0),
        name="own_sum",
    )(slots, a, b)


def unit_kernel(tokens, chunks, row_ref, a_ref, b_ref, out_ref, total):
    total[...] = a_ref[...] + b_ref[...]
    out_ref[...] = jnp.zeros_like(out_ref)
    count = total.shape[0] // tokens
    half = LANES // 2
    width = chunks * LANES
    low = lax.broadcasted_iota(jnp.int32, (chunks, LANES), 1) < half
    low_t = lax.broadcasted_iota(jnp.int32, (tokens, LANES), 1) < half

    @pl.loop(0, count, unroll=4)
    def _(i):
        part = total[pl.ds(pl.multiple_of(i * tokens, 8), tokens), :]
        twice = jnp.where(low_t, pltpu.roll(part, half, 1), part)
        g_hi = part.astype(jnp.bfloat16).astype(jnp.float32)
        a_hi = twice.astype(jnp.bfloat16).astype(jnp.float32)
        left = jnp.concatenate([g_hi, g_hi, part - g_hi], axis=0)[:, :half].astype(jnp.bfloat16)
        right = jnp.concatenate([a_hi, twice - a_hi, a_hi], axis=0).astype(jnp.bfloat16)
        prod = lax.dot_general(left, right, TN, preferred_element_type=jnp.float32)
        entries = jnp.where(low, prod[:chunks], prod[chunks : 2 * chunks])
        square = jnp.sum(entries * entries, axis=0, keepdims=True)
        mean = jnp.sum(square, axis=1, keepdims=True) / width
        unit = (entries * lax.rsqrt(mean + epsilon)).astype(jnp.bfloat16)
        row = pl.multiple_of(row_ref[i] * chunks, chunks)
        out_ref[pl.ds(row, chunks), :] = unit


def unit_grads(slots, a, b, tokens, chunks, slot_count):
    whole = pl.BlockSpec(memory_space=pltpu.VMEM)
    return pl.pallas_call(
        functools.partial(unit_kernel, tokens, chunks),
        in_specs=[pl.BlockSpec(memory_space=pltpu.SMEM), whole, whole],
        out_specs=whole,
        out_shape=jax.ShapeDtypeStruct((slot_count * chunks, LANES), jnp.bfloat16),
        scratch_shapes=[pltpu.VMEM(a.shape, jnp.float32)],
        compiler_params=pltpu.CompilerParams(vmem_limit_bytes=16 << 20),
        cost_estimate=pl.CostEstimate(flops=20_000_000, bytes_accessed=1_000_000, transcendentals=0),
        name="unit_grads",
    )(slots, a, b)


def stage_units(refs, stage, parts, slots, groups):
    each = stage.shape[1] // (len(refs) * groups * slots)
    span = slots * parts * each

    @pl.loop(0, groups)
    def _(d):
        for n, ref in enumerate(refs):
            got = ref[pl.ds(pl.multiple_of(d * span, span), span), :].astype(jnp.float32)
            got = got.reshape(slots, parts, each, LANES)
            for k in range(parts):
                at = pl.multiple_of((n * groups + d) * slots * each, each)
                stage[k, pl.ds(at, slots * each), :] = got[:, k].reshape(slots * each, LANES)


def staged_rows(stage, k, units, at):
    rows = units.shape[0] - at
    each = units.shape[1] // LANES
    for j in range(each):
        piece = stage[k, pl.ds(j, rows, stride=each), :]
        units[at:, j * LANES : (j + 1) * LANES] = piece.astype(jnp.bfloat16)


def stage_kernel(groups, slots, x0_ref, x1_ref, q_hbm, out_ref, held_ref, stage, sems):
    parts, _, width = held_ref.shape

    def load(k):
        columns = q_hbm.at[:, pl.ds(k * width, width)]
        return pltpu.make_async_copy(columns, held_ref.at[k], sems.at[k])

    for k in range(parts):
        load(k).start()
    stage_units((x0_ref, x1_ref), stage, parts, slots, groups)

    @pl.loop(0, parts)
    def _(k):
        staged_rows(stage, k, out_ref.at[k], 0)

    for k in range(parts):
        load(k).wait()


def staged(x0, x1, queries, groups, slots, parts):
    rows = 2 * groups * slots
    count, width = queries.shape[0], queries.shape[1] // parts
    vmem = pl.BlockSpec(memory_space=pltpu.VMEM)
    return pl.pallas_call(
        functools.partial(stage_kernel, groups, slots),
        in_specs=[vmem, vmem, pl.BlockSpec(memory_space=pltpu.HBM)],
        out_specs=[vmem] * 2,
        out_shape=[
            jax.ShapeDtypeStruct((parts, rows, width), jnp.bfloat16),
            jax.ShapeDtypeStruct((parts, count, width), jnp.bfloat16),
        ],
        scratch_shapes=[
            pltpu.VMEM((parts, rows * width // LANES, LANES), jnp.float32),
            pltpu.SemaphoreType.DMA((parts,)),
        ],
        compiler_params=pltpu.CompilerParams(vmem_limit_bytes=16 << 20),
        cost_estimate=pl.CostEstimate(
            flops=4 * x0.size, bytes_accessed=4 * queries.size, transcendentals=0
        ),
        name="staged",
    )(x0, x1, queries)


def score_kernel(groups, slots, padded, x0_ref, x1_ref, early_ref, q_ref, out_ref, stage, units, total):
    parts = q_ref.shape[0]
    half = groups * slots
    stage_units((x0_ref, x1_ref), stage, parts, slots, groups)
    total[...] = jnp.zeros_like(total)

    @pl.loop(0, parts)
    def _(k):
        units[0 : 2 * half, :] = early_ref[k]
        staged_rows(stage, k, units, 2 * half)
        total[...] += lax.dot_general(q_ref[k], units[...], NT, preferred_element_type=jnp.float32)

    row = lax.broadcasted_iota(jnp.int32, (groups * padded, 4 * half), 0)
    column = lax.broadcasted_iota(jnp.int32, (1, 4 * half), 1)
    place = column
    for n in range(1, 4):
        place += jnp.where(column >= n * half, slots - half, 0)
    for n in range(4):
        for d in range(1, groups):
            after = (column >= n * half + d * slots) & (column < (n + 1) * half)
            place += jnp.where(after, padded - slots, 0)
    pick = jnp.where(row == place, 1.0, 0.0).astype(jnp.bfloat16)
    out = lax.dot_general(
        pick, total[...].astype(jnp.bfloat16), NT, preferred_element_type=jnp.float32
    )
    out_ref[...] = out.astype(out_ref.dtype)


def scores_of(x0, x1, early, queries, groups, slots, padded):
    parts, count, width = queries.shape
    half = groups * slots
    vmem = pl.BlockSpec(memory_space=pltpu.VMEM)
    return pl.pallas_call(
        functools.partial(score_kernel, groups, slots, padded),
        in_specs=[vmem] * 4,
        out_specs=vmem,
        out_shape=jax.ShapeDtypeStruct((groups * padded, count), jnp.bfloat16),
        scratch_shapes=[
            pltpu.VMEM((parts, 2 * half * width // LANES, LANES), jnp.float32),
            pltpu.VMEM((4 * half, width), jnp.bfloat16),
            pltpu.VMEM((count, 4 * half), jnp.float32),
        ],
        compiler_params=pltpu.CompilerParams(vmem_limit_bytes=24 << 20),
        cost_estimate=pl.CostEstimate(
            flops=2 * 4 * half * queries.size, bytes_accessed=2 * queries.size, transcendentals=0
        ),
        name="scores",
    )(x0, x1, early, queries)


def pick_kernel(row_ref, x_ref, out_ref):
    count = row_ref.shape[1]
    rows = x_ref.shape[0]
    parts = x_ref.shape[1] // LANES
    hit = lax.broadcasted_iota(jnp.int32, (rows, count), 0) == row_ref[...]
    pick = jnp.where(hit, 1.0, 0.0).T.astype(jnp.bfloat16)
    got = jnp.dot(pick, x_ref[...], preferred_element_type=jnp.float32)
    for j in range(parts):
        out_ref[pl.ds(j, count, stride=parts), :] = got[:, j * LANES : (j + 1) * LANES]


def pick_rows(row, x):
    vmem = pl.BlockSpec(memory_space=pltpu.VMEM)
    count, width = row.shape[1], x.shape[1]
    return pl.pallas_call(
        pick_kernel,
        in_specs=[vmem, vmem],
        out_specs=vmem,
        out_shape=jax.ShapeDtypeStruct((count * (width // LANES), LANES), jnp.float32),
        compiler_params=pltpu.CompilerParams(vmem_limit_bytes=16 << 20),
        cost_estimate=pl.CostEstimate(flops=16_000_000, bytes_accessed=400_000, transcendentals=0),
        name="pick_rows",
    )(row, x)


def local_one(activations, out_grads, proj_in, proj_out, queries, candidates):
    examples, tokens, hidden = activations.shape
    features = out_grads.shape[2]
    groups = lax.axis_size("dp")
    ways = lax.axis_size("tensor")
    capacity = max(2, 5 * examples // (2 * groups))
    slots = -(-capacity // ways)
    padded = -(-ways * slots // 8) * 8
    query_block = queries[0]
    chunks = query_block.shape[1] // LANES
    core = [(i, i ^ 1) for i in range(ways)]
    across = [(i, i ^ 2) for i in range(ways)]

    own_part, over_part, near_part, far_part, my_slots, pick = project(
        candidates.reshape(1, examples),
        activations.reshape(examples * tokens, hidden),
        out_grads.reshape(examples * tokens, features),
        proj_in.T,
        proj_out.T,
        tokens,
        groups,
        ways,
        slots,
        padded,
    )
    far_in = lax.ppermute(far_part, "tensor", core)
    near_in = lax.ppermute(near_part, "tensor", core)
    across_in = lax.ppermute(over_part + far_in, "tensor", across)

    here_slots, here = own_sum(my_slots, own_part, near_in, examples // ways)
    units = unit_grads(here_slots, here, across_in, tokens, chunks, groups * slots)
    shape = (groups, slots * chunks, LANES)
    own = lax.all_to_all(units.reshape(shape), "dp", split_axis=0, concat_axis=0, tiled=True)
    own = own.reshape(units.shape)
    over_y = lax.ppermute(own, "tensor", across)
    over_core = lax.ppermute(own, "tensor", core)
    early, held = staged(own, over_core, query_block, groups, slots, 4)
    over_y, early = lax.optimization_barrier((over_y, early))
    over_both = lax.ppermute(over_y, "tensor", core)
    both = scores_of(over_y, over_both, early, held, groups, slots, padded)
    block = both.reshape(groups, padded, both.shape[1])
    returned = lax.all_to_all(block, "dp", split_axis=0, concat_axis=0, tiled=True)
    picked = pick_rows(pick, returned.reshape(both.shape))
    return picked.reshape(examples, 1, both.shape[1])


def local_many(activations, out_grads, proj_in, proj_out, queries, candidates):
    examples_here, tokens_here, hidden_here = activations.shape
    proj_rank = proj_in.shape[1]
    per_example = candidates.shape[1]
    groups = lax.axis_size("dp")
    capacity = max(2, 5 * examples_here * per_example // (2 * groups))
    act_proj = jnp.dot(
        activations.reshape(examples_here * tokens_here, hidden_here),
        proj_in,
        preferred_element_type=jnp.float32,
    )
    grad_proj = jnp.dot(
        out_grads.reshape(examples_here * tokens_here, out_grads.shape[2]),
        proj_out,
        preferred_element_type=jnp.float32,
    )
    both_proj = jnp.concatenate([grad_proj, act_proj], axis=1).reshape(
        examples_here, tokens_here, 2 * proj_rank
    )
    summed = lax.psum(both_proj, "tensor")
    grad_side = summed[:, :, :proj_rank]
    act_side = summed[:, :, proj_rank:]
    example_grads = jnp.einsum(
        "eta,etb->eab", grad_side, act_side, precision=lax.Precision.HIGHEST
    ).reshape(examples_here, proj_rank * proj_rank)
    inv_rms = lax.rsqrt(jnp.mean(example_grads * example_grads, axis=1, keepdims=True) + epsilon)
    unit = (example_grads * inv_rms).astype(jnp.bfloat16)
    flat_cands = candidates.reshape(-1)
    hit_table = (flat_cands[:, None] == jnp.arange(groups, dtype=jnp.int32)[None, :]).astype(
        jnp.int32
    )
    earlier = jnp.cumsum(hit_table, axis=0) - hit_table
    slot_index = jnp.sum(earlier * hit_table, axis=1)
    dest_index = flat_cands * capacity + slot_index
    row_copies = jnp.repeat(unit, per_example, axis=0)
    grad_width = unit.shape[1]
    send_buffer = (
        jnp.zeros((groups * capacity, grad_width), jnp.bfloat16).at[dest_index].set(row_copies)
    )
    send_buffer = send_buffer.reshape(groups, capacity, grad_width)
    col_width = grad_width // lax.axis_size("tensor")
    column_part = lax.dynamic_slice_in_dim(
        send_buffer, lax.axis_index("tensor") * col_width, col_width, 2
    )
    received = lax.all_to_all(column_part, "dp", split_axis=0, concat_axis=0, tiled=True)
    slot_scores = jnp.einsum(
        "gsk,qk->gsq",
        lax.all_gather(received, "tensor", axis=2, tiled=True),
        queries[0],
        preferred_element_type=jnp.float32,
    )
    returned = lax.all_to_all(slot_scores, "dp", split_axis=0, concat_axis=0, tiled=True)
    picked = returned.reshape(groups * capacity, returned.shape[2])[dest_index]
    return picked.reshape(examples_here, per_example, returned.shape[2])


def local(activations, out_grads, proj_in, proj_out, queries, candidates):
    one = candidates.shape[1] == 1 and lax.axis_size("tensor") == 4
    return (local_one if one else local_many)(
        activations, out_grads, proj_in, proj_out, queries, candidates
    )


def solution(mesh):
    placed = (
        P("dp", None, "tensor"),
        P("dp", None, "tensor"),
        P("tensor", None),
        P("tensor", None),
        P("dp", "tensor", None),
        P("dp", None),
    )
    return jax.shard_map(
        local, mesh=mesh, in_specs=placed, out_specs=P("dp", None, "tensor"), check_vma=False
    )
```

```python
import functools

import jax
import jax.numpy as jnp
from jax import lax
from jax.experimental import pallas as pl
from jax.experimental.pallas import tpu as pltpu
from jax.sharding import PartitionSpec as P

epsilon = 1e-06
LANES = 128
NT = (((1,), (1,)), ((), ()))
TN = (((0,), (0,)), ((), ()))


def project_kernel(
    groups, ways, tokens, slots, padded, blocks,
    cand_hbm, act_hbm, grad_hbm, win_hbm, wout_hbm,
    own_ref, over_ref, near_ref, far_ref, slot_ref, pick_ref,
    act, grad, win, wout, raw, dealt, cand, rank, start, act_sems, grad_sems, sems,
):
    proj_rank = win.shape[0]
    examples = cand.shape[1]
    share = examples // ways
    step = act.shape[0] // act_sems.shape[0]
    me = lax.axis_index("tensor")
    home = lax.axis_index("dp")

    def piece(i):
        return pl.ds(pl.multiple_of(i * step, step), step)

    def act_copy(i):
        return pltpu.make_async_copy(act_hbm.at[piece(i)], act.at[piece(i)], act_sems.at[i])

    def grad_copy(i):
        return pltpu.make_async_copy(grad_hbm.at[piece(i)], grad.at[piece(i)], grad_sems.at[i])

    cand_copy = pltpu.make_async_copy(cand_hbm, cand, sems.at[0])
    raw_copy = pltpu.make_async_copy(wout_hbm, raw, sems.at[1])
    win_copy = pltpu.make_async_copy(win_hbm, win, sems.at[2])
    cand_copy.start()
    raw_copy.start()
    win_copy.start()

    @pl.loop(0, act_sems.shape[0])
    def _(i):
        act_copy(i).start()
        grad_copy(i).start()

    cand_copy.wait()

    @pl.loop(0, groups)
    def _(g):
        start[g] = 0

    @pl.loop(0, examples)
    def _(e):
        g = cand[0, e]
        rank[e] = start[g]
        start[g] = start[g] + 1

    def shift(g, below):
        here = start[g]
        start[g] = below
        return below + here

    lax.fori_loop(0, groups, shift, jnp.int32(0))

    half = proj_rank // 2
    r = lax.broadcasted_iota(jnp.int32, (proj_rank, proj_rank), 0)
    c = lax.broadcasted_iota(jnp.int32, (proj_rank, proj_rank), 1)
    pick = (c == jnp.where(r < half, 2 * r, 2 * (r - half) + 1)).astype(jnp.bfloat16)
    raw_copy.wait()
    wout[...] = jnp.dot(pick, raw[...], preferred_element_type=jnp.float32).astype(jnp.bfloat16)
    win_copy.wait()

    done = 0
    for count, rows in blocks:

        @pl.loop(0, count)
        def _(i, done=done, rows=rows):
            for j in range(rows // step):
                act_copy(done // step + i * (rows // step) + j).wait()
                grad_copy(done // step + i * (rows // step) + j).wait()
            at = pl.multiple_of(done + i * rows, step)
            here = pl.ds(at, rows)
            left = lax.dot_general(grad[here, :], wout[...], NT, preferred_element_type=jnp.float32)
            right = lax.dot_general(act[here, :], win[...], NT, preferred_element_type=jnp.float32)
            both = jnp.concatenate([left, right], axis=1)
            first = done // tokens + i * (rows // tokens)
            for k in range(rows // tokens):
                e = first + k
                g = cand[0, e]
                place = start[g] + rank[e]
                owner = place & (ways - 1)
                turn = place >> (ways.bit_length() - 1)
                before = (start[g] + ways - 1 - owner) >> (ways.bit_length() - 1)
                rel = owner ^ me
                slot_ref[rel * share + turn] = (g ^ home) * slots + turn - before
                pick_ref[0, e] = g * padded + rel * slots + turn - before
                row = (rel * share + turn) * tokens
                dealt[pl.ds(pl.multiple_of(row, 8), tokens), :] = both[
                    k * tokens : (k + 1) * tokens
                ]

        done += count * rows

    size = share * tokens
    for r, ref in enumerate((own_ref, near_ref, over_ref, far_ref)):
        ref[...] = dealt[r * size : (r + 1) * size, :]


def project(cands, act, grad, win, wout, tokens, groups, ways, slots, padded):
    examples = cands.shape[1]
    rows = act.shape[0]
    pieces = 8
    step = rows // pieces
    blocks = ((3, 2 * step), (2, step))
    share = rows // ways
    hbm = pl.BlockSpec(memory_space=pltpu.HBM)
    vmem = pl.BlockSpec(memory_space=pltpu.VMEM)
    return pl.pallas_call(
        functools.partial(project_kernel, groups, ways, tokens, slots, padded, blocks),
        in_specs=[hbm] * 5,
        out_specs=[vmem] * 4 + [pl.BlockSpec(memory_space=pltpu.SMEM)] * 2,
        out_shape=[pltpu.VMEM((share, LANES), jnp.float32)] * 4
        + [
            pltpu.SMEM((examples,), jnp.int32),
            jax.ShapeDtypeStruct((1, examples), jnp.int32),
        ],
        scratch_shapes=[
            pltpu.VMEM(act.shape, jnp.bfloat16),
            pltpu.VMEM(grad.shape, jnp.bfloat16),
            pltpu.VMEM(win.shape, jnp.bfloat16),
            pltpu.VMEM(wout.shape, jnp.bfloat16),
            pltpu.VMEM(wout.shape, jnp.bfloat16),
            pltpu.VMEM((rows, LANES), jnp.float32),
            pltpu.SMEM((1, examples), jnp.int32),
            pltpu.SMEM((examples,), jnp.int32),
            pltpu.SMEM((groups,), jnp.int32),
            pltpu.SemaphoreType.DMA((pieces,)),
            pltpu.SemaphoreType.DMA((pieces,)),
            pltpu.SemaphoreType.DMA((3,)),
        ],
        compiler_params=pltpu.CompilerParams(vmem_limit_bytes=61 << 20),
        cost_estimate=pl.CostEstimate(
            flops=2 * rows * (act.shape[1] + grad.shape[1]) * 64,
            bytes_accessed=2 * rows * (act.shape[1] + grad.shape[1]),
            transcendentals=0,
        ),
        name="project",
    )(cands, act, grad, win, wout)


def own_kernel(slot_ref, a_ref, b_ref, q_hbm, out_slot_ref, out_ref, held_ref, sems):
    parts, _, width = held_ref.shape

    def load(k):
        columns = q_hbm.at[:, pl.ds(k * width, width)]
        return pltpu.make_async_copy(columns, held_ref.at[k], sems.at[k])

    for k in range(parts):
        load(k).start()
    out_ref[...] = a_ref[...] + b_ref[...]

    @pl.loop(0, out_slot_ref.shape[0])
    def _(i):
        out_slot_ref[i] = slot_ref[i]

    for k in range(parts):
        load(k).wait()


def own_sum(slots, a, b, queries, count, parts):
    smem = pl.BlockSpec(memory_space=pltpu.SMEM)
    vmem = pl.BlockSpec(memory_space=pltpu.VMEM)
    return pl.pallas_call(
        own_kernel,
        in_specs=[smem, vmem, vmem, pl.BlockSpec(memory_space=pltpu.HBM)],
        out_specs=[smem, vmem, vmem],
        out_shape=[
            pltpu.SMEM((count,), jnp.int32),
            pltpu.VMEM(a.shape, a.dtype),
            pltpu.VMEM((parts, queries.shape[0], queries.shape[1] // parts), queries.dtype),
        ],
        scratch_shapes=[pltpu.SemaphoreType.DMA((parts,))],
        compiler_params=pltpu.CompilerParams(vmem_limit_bytes=48 << 20),
        cost_estimate=pl.CostEstimate(
            flops=a.size, bytes_accessed=2 * queries.size, transcendentals=0
        ),
        name="own_sum",
    )(slots, a, b, queries)


def unit_kernel(tokens, chunks, row_ref, a_ref, b_ref, *rest):
    out_refs, total, units = rest[:-2], rest[-2], rest[-1]
    total[...] = a_ref[...] + b_ref[...]
    units[...] = jnp.zeros_like(units)
    count = total.shape[0] // tokens
    half = LANES // 2
    width = chunks * LANES
    low = lax.broadcasted_iota(jnp.int32, (chunks, LANES), 1) < half
    low_t = lax.broadcasted_iota(jnp.int32, (tokens, LANES), 1) < half

    @pl.loop(0, count, unroll=4)
    def _(i):
        part = total[pl.ds(pl.multiple_of(i * tokens, 8), tokens), :]
        twice = jnp.where(low_t, pltpu.roll(part, half, 1), part)
        g_hi = part.astype(jnp.bfloat16).astype(jnp.float32)
        a_hi = twice.astype(jnp.bfloat16).astype(jnp.float32)
        left = jnp.concatenate([g_hi, g_hi, part - g_hi], axis=0)[:, :half].astype(jnp.bfloat16)
        right = jnp.concatenate([a_hi, twice - a_hi, a_hi], axis=0).astype(jnp.bfloat16)
        prod = lax.dot_general(left, right, TN, preferred_element_type=jnp.float32)
        entries = jnp.where(low, prod[:chunks], prod[chunks : 2 * chunks])
        square = jnp.sum(entries * entries, axis=0, keepdims=True)
        mean = jnp.sum(square, axis=1, keepdims=True) / width
        unit = (entries * lax.rsqrt(mean + epsilon)).astype(jnp.bfloat16)
        row = pl.multiple_of(row_ref[i] * chunks, chunks)
        units[pl.ds(row, chunks), :] = unit

    for n, ref in enumerate(out_refs):
        size = ref.shape[0]
        ref[...] = units[n * size : (n + 1) * size, :]


def unit_grads(slots, a, b, tokens, chunks, groups, slot_count):
    rows = slot_count * chunks
    whole = pl.BlockSpec(memory_space=pltpu.VMEM)
    return pl.pallas_call(
        functools.partial(unit_kernel, tokens, chunks),
        in_specs=[pl.BlockSpec(memory_space=pltpu.SMEM), whole, whole],
        out_specs=[whole] * groups,
        out_shape=[jax.ShapeDtypeStruct((rows, LANES), jnp.bfloat16)] * groups,
        scratch_shapes=[
            pltpu.VMEM(a.shape, jnp.float32),
            pltpu.VMEM((groups * rows, LANES), jnp.bfloat16),
        ],
        compiler_params=pltpu.CompilerParams(vmem_limit_bytes=16 << 20),
        cost_estimate=pl.CostEstimate(flops=20_000_000, bytes_accessed=1_000_000, transcendentals=0),
        name="unit_grads",
    )(slots, a, b)


def stage_units(refs, stage, parts, slots, groups):
    each = stage.shape[1] // (len(refs) // 2 * groups * slots)
    span = slots * parts * each
    home = lax.axis_index("dp")

    @pl.loop(0, groups // 2)
    def _(i):
        for n, ref in enumerate(refs):
            d = (2 * i + n % 2) ^ home
            got = ref[pl.ds(pl.multiple_of(i * span, span), span), :].astype(jnp.float32)
            got = got.reshape(slots, parts, each, LANES)
            for k in range(parts):
                at = pl.multiple_of((n // 2 * groups + d) * slots * each, each)
                stage[k, pl.ds(at, slots * each), :] = got[:, k].reshape(slots * each, LANES)


def staged_rows(stage, k, units, at):
    rows = units.shape[0] - at
    each = units.shape[1] // LANES
    for j in range(each):
        piece = stage[k, pl.ds(j, rows, stride=each), :]
        units[at:, j * LANES : (j + 1) * LANES] = piece.astype(jnp.bfloat16)


def stage_kernel(groups, slots, *rest):
    refs, (out_ref, stage) = rest[:4], rest[4:]
    parts = out_ref.shape[0]
    stage_units(refs, stage, parts, slots, groups)

    @pl.loop(0, parts)
    def _(k):
        staged_rows(stage, k, out_ref.at[k], 0)


def staged(units, groups, slots, parts):
    rows = 2 * groups * slots
    width = 2 * units[0].size // (groups * slots * parts)
    vmem = pl.BlockSpec(memory_space=pltpu.VMEM)
    return pl.pallas_call(
        functools.partial(stage_kernel, groups, slots),
        in_specs=[vmem] * 4,
        out_specs=vmem,
        out_shape=pltpu.VMEM((parts, rows, width), jnp.bfloat16),
        scratch_shapes=[pltpu.VMEM((parts, rows * width // LANES, LANES), jnp.float32)],
        compiler_params=pltpu.CompilerParams(vmem_limit_bytes=16 << 20),
        cost_estimate=pl.CostEstimate(
            flops=rows * parts * width, bytes_accessed=8 * rows * width, transcendentals=0
        ),
        name="staged",
    )(*units)


def score_kernel(groups, slots, padded, *rest):
    refs, (early_ref, q_ref, out_ref, stage, units, total) = rest[:4], rest[4:]
    parts = q_ref.shape[0]
    half = groups * slots
    stage_units(refs, stage, parts, slots, groups)
    total[...] = jnp.zeros_like(total)

    @pl.loop(0, parts)
    def _(k):
        units[0 : 2 * half, :] = early_ref[k]
        staged_rows(stage, k, units, 2 * half)
        total[...] += lax.dot_general(q_ref[k], units[...], NT, preferred_element_type=jnp.float32)

    row = lax.broadcasted_iota(jnp.int32, (groups * padded, 4 * half), 0)
    column = lax.broadcasted_iota(jnp.int32, (1, 4 * half), 1)
    place = column
    for n in range(1, 4):
        place += jnp.where(column >= n * half, slots - half, 0)
    for n in range(4):
        for d in range(1, groups):
            after = (column >= n * half + d * slots) & (column < (n + 1) * half)
            place += jnp.where(after, padded - slots, 0)
    pick = jnp.where(row == place, 1.0, 0.0).astype(jnp.bfloat16)
    out = lax.dot_general(
        pick, total[...].astype(jnp.bfloat16), NT, preferred_element_type=jnp.float32
    )
    out_ref[...] = out.astype(out_ref.dtype)


def scores_of(late, early, queries, groups, slots, padded):
    parts, count, width = queries.shape
    half = groups * slots
    vmem = pl.BlockSpec(memory_space=pltpu.VMEM)
    return pl.pallas_call(
        functools.partial(score_kernel, groups, slots, padded),
        in_specs=[vmem] * 6,
        out_specs=vmem,
        out_shape=jax.ShapeDtypeStruct((groups * padded, count), jnp.bfloat16),
        scratch_shapes=[
            pltpu.VMEM((parts, 2 * half * width // LANES, LANES), jnp.float32),
            pltpu.VMEM((4 * half, width), jnp.bfloat16),
            pltpu.VMEM((count, 4 * half), jnp.float32),
        ],
        compiler_params=pltpu.CompilerParams(vmem_limit_bytes=24 << 20),
        cost_estimate=pl.CostEstimate(
            flops=2 * 4 * half * queries.size, bytes_accessed=2 * queries.size, transcendentals=0
        ),
        name="scores",
    )(*late, early, queries)


def pick_kernel(row_ref, x_ref, out_ref):
    count = row_ref.shape[1]
    rows = x_ref.shape[0]
    parts = x_ref.shape[1] // LANES
    hit = lax.broadcasted_iota(jnp.int32, (rows, count), 0) == row_ref[...]
    pick = jnp.where(hit, 1.0, 0.0).T.astype(jnp.bfloat16)
    got = jnp.dot(pick, x_ref[...], preferred_element_type=jnp.float32)
    for j in range(parts):
        out_ref[pl.ds(j, count, stride=parts), :] = got[:, j * LANES : (j + 1) * LANES]


def pick_rows(row, x):
    vmem = pl.BlockSpec(memory_space=pltpu.VMEM)
    count, width = row.shape[1], x.shape[1]
    return pl.pallas_call(
        pick_kernel,
        in_specs=[vmem, vmem],
        out_specs=vmem,
        out_shape=jax.ShapeDtypeStruct((count * (width // LANES), LANES), jnp.float32),
        compiler_params=pltpu.CompilerParams(vmem_limit_bytes=16 << 20),
        cost_estimate=pl.CostEstimate(flops=16_000_000, bytes_accessed=400_000, transcendentals=0),
        name="pick_rows",
    )(row, x)


def local_one(activations, out_grads, proj_in, proj_out, queries, candidates):
    examples, tokens, hidden = activations.shape
    features = out_grads.shape[2]
    groups = lax.axis_size("dp")
    ways = lax.axis_size("tensor")
    capacity = max(2, 5 * examples // (2 * groups))
    slots = -(-capacity // ways)
    padded = -(-ways * slots // 8) * 8
    query_block = queries[0]
    chunks = query_block.shape[1] // LANES
    core = [(i, i ^ 1) for i in range(ways)]
    across = [(i, i ^ 2) for i in range(ways)]

    own_part, over_part, near_part, far_part, my_slots, pick = project(
        candidates.reshape(1, examples),
        activations.reshape(examples * tokens, hidden),
        out_grads.reshape(examples * tokens, features),
        proj_in.T,
        proj_out.T,
        tokens,
        groups,
        ways,
        slots,
        padded,
    )
    far_in = lax.ppermute(far_part, "tensor", core)
    near_in = lax.ppermute(near_part, "tensor", core)
    across_in = lax.ppermute(over_part + far_in, "tensor", across)

    here_slots, here, held = own_sum(
        my_slots, own_part, near_in, query_block, examples // ways, 4
    )
    units = unit_grads(here_slots, here, across_in, tokens, chunks, groups, slots)
    arrived = [units[0]] + [None] * (groups - 1)
    for k in reversed(range(1, groups)):
        arrived[k] = lax.ppermute(units[k], "dp", [(i, i ^ k) for i in range(groups)])
    own = [jnp.concatenate(arrived[n::2], axis=0) for n in range(2)]
    over_y = [lax.ppermute(x, "tensor", across) for x in own]
    over_core = [lax.ppermute(x, "tensor", core) for x in own]
    early = staged(own + over_core, groups, slots, held.shape[0])
    over_both = [lax.ppermute(x, "tensor", core) for x in over_y]
    both = scores_of(over_y + over_both, early, held, groups, slots, padded)
    block = both.reshape(groups, padded, both.shape[1])
    returned = lax.all_to_all(block, "dp", split_axis=0, concat_axis=0, tiled=True)
    picked = pick_rows(pick, returned.reshape(both.shape))
    return picked.reshape(examples, 1, both.shape[1])


def local_many(activations, out_grads, proj_in, proj_out, queries, candidates):
    examples_here, tokens_here, hidden_here = activations.shape
    proj_rank = proj_in.shape[1]
    per_example = candidates.shape[1]
    groups = lax.axis_size("dp")
    capacity = max(2, 5 * examples_here * per_example // (2 * groups))
    act_proj = jnp.dot(
        activations.reshape(examples_here * tokens_here, hidden_here),
        proj_in,
        preferred_element_type=jnp.float32,
    )
    grad_proj = jnp.dot(
        out_grads.reshape(examples_here * tokens_here, out_grads.shape[2]),
        proj_out,
        preferred_element_type=jnp.float32,
    )
    both_proj = jnp.concatenate([grad_proj, act_proj], axis=1).reshape(
        examples_here, tokens_here, 2 * proj_rank
    )
    summed = lax.psum(both_proj, "tensor")
    grad_side = summed[:, :, :proj_rank]
    act_side = summed[:, :, proj_rank:]
    example_grads = jnp.einsum(
        "eta,etb->eab", grad_side, act_side, precision=lax.Precision.HIGHEST
    ).reshape(examples_here, proj_rank * proj_rank)
    inv_rms = lax.rsqrt(jnp.mean(example_grads * example_grads, axis=1, keepdims=True) + epsilon)
    unit = (example_grads * inv_rms).astype(jnp.bfloat16)
    flat_cands = candidates.reshape(-1)
    hit_table = (flat_cands[:, None] == jnp.arange(groups, dtype=jnp.int32)[None, :]).astype(
        jnp.int32
    )
    earlier = jnp.cumsum(hit_table, axis=0) - hit_table
    slot_index = jnp.sum(earlier * hit_table, axis=1)
    dest_index = flat_cands * capacity + slot_index
    row_copies = jnp.repeat(unit, per_example, axis=0)
    grad_width = unit.shape[1]
    send_buffer = (
        jnp.zeros((groups * capacity, grad_width), jnp.bfloat16).at[dest_index].set(row_copies)
    )
    send_buffer = send_buffer.reshape(groups, capacity, grad_width)
    col_width = grad_width // lax.axis_size("tensor")
    column_part = lax.dynamic_slice_in_dim(
        send_buffer, lax.axis_index("tensor") * col_width, col_width, 2
    )
    received = lax.all_to_all(column_part, "dp", split_axis=0, concat_axis=0, tiled=True)
    slot_scores = jnp.einsum(
        "gsk,qk->gsq",
        lax.all_gather(received, "tensor", axis=2, tiled=True),
        queries[0],
        preferred_element_type=jnp.float32,
    )
    returned = lax.all_to_all(slot_scores, "dp", split_axis=0, concat_axis=0, tiled=True)
    picked = returned.reshape(groups * capacity, returned.shape[2])[dest_index]
    return picked.reshape(examples_here, per_example, returned.shape[2])


def local(activations, out_grads, proj_in, proj_out, queries, candidates):
    one = candidates.shape[1] == 1 and lax.axis_size("tensor") == 4
    return (local_one if one else local_many)(
        activations, out_grads, proj_in, proj_out, queries, candidates
    )


def solution(mesh):
    placed = (
        P("dp", None, "tensor"),
        P("dp", None, "tensor"),
        P("tensor", None),
        P("tensor", None),
        P("dp", "tensor", None),
        P("dp", None),
    )
    return jax.shard_map(
        local, mesh=mesh, in_specs=placed, out_specs=P("dp", None, "tensor"), check_vma=False
    )
```

```python
import functools

import jax
import jax.numpy as jnp
from jax import lax
from jax.experimental import pallas as pl
from jax.experimental.pallas import tpu as pltpu
from jax.sharding import PartitionSpec as P

epsilon = 1e-06
LANES = 128
NT = (((1,), (1,)), ((), ()))
TN = (((0,), (0,)), ((), ()))


def project_kernel(
    groups, ways, tokens, slots, padded, blocks,
    cand_hbm, act_hbm, grad_hbm, win_hbm, wout_hbm,
    own_ref, over_ref, near_ref, far_ref, slot_ref, pick_ref,
    act, grad, win, wout, raw, dealt, cand, rank, start, act_sems, grad_sems, sems,
):
    proj_rank = win.shape[0]
    examples = cand.shape[1]
    share = examples // ways
    step = act.shape[0] // act_sems.shape[0]
    me = lax.axis_index("tensor")
    home = lax.axis_index("dp")

    def piece(i):
        return pl.ds(pl.multiple_of(i * step, step), step)

    def act_copy(i):
        return pltpu.make_async_copy(act_hbm.at[piece(i)], act.at[piece(i)], act_sems.at[i])

    def grad_copy(i):
        return pltpu.make_async_copy(grad_hbm.at[piece(i)], grad.at[piece(i)], grad_sems.at[i])

    cand_copy = pltpu.make_async_copy(cand_hbm, cand, sems.at[0])
    raw_copy = pltpu.make_async_copy(wout_hbm, raw, sems.at[1])
    win_copy = pltpu.make_async_copy(win_hbm, win, sems.at[2])
    cand_copy.start()
    raw_copy.start()
    win_copy.start()

    @pl.loop(0, act_sems.shape[0])
    def _(i):
        act_copy(i).start()
        grad_copy(i).start()

    cand_copy.wait()

    @pl.loop(0, groups)
    def _(g):
        start[g] = 0

    @pl.loop(0, examples)
    def _(e):
        g = cand[0, e]
        rank[e] = start[g]
        start[g] = start[g] + 1

    def shift(g, below):
        here = start[g]
        start[g] = below
        return below + here

    lax.fori_loop(0, groups, shift, jnp.int32(0))

    half = proj_rank // 2
    r = lax.broadcasted_iota(jnp.int32, (proj_rank, proj_rank), 0)
    c = lax.broadcasted_iota(jnp.int32, (proj_rank, proj_rank), 1)
    pick = (c == jnp.where(r < half, 2 * r, 2 * (r - half) + 1)).astype(jnp.bfloat16)
    raw_copy.wait()
    wout[...] = jnp.dot(pick, raw[...], preferred_element_type=jnp.float32).astype(jnp.bfloat16)
    win_copy.wait()

    done = 0
    for count, rows in blocks:

        @pl.loop(0, count)
        def _(i, done=done, rows=rows):
            for j in range(rows // step):
                act_copy(done // step + i * (rows // step) + j).wait()
                grad_copy(done // step + i * (rows // step) + j).wait()
            at = pl.multiple_of(done + i * rows, step)
            here = pl.ds(at, rows)
            left = lax.dot_general(grad[here, :], wout[...], NT, preferred_element_type=jnp.float32)
            right = lax.dot_general(act[here, :], win[...], NT, preferred_element_type=jnp.float32)
            both = jnp.concatenate([left, right], axis=1)
            first = done // tokens + i * (rows // tokens)
            for k in range(rows // tokens):
                e = first + k
                g = cand[0, e]
                place = start[g] + rank[e]
                owner = place & (ways - 1)
                turn = place >> (ways.bit_length() - 1)
                before = (start[g] + ways - 1 - owner) >> (ways.bit_length() - 1)
                rel = owner ^ me
                slot_ref[rel * share + turn] = (g ^ home) * slots + turn - before
                pick_ref[0, e] = g * padded + rel * slots + turn - before
                row = (rel * share + turn) * tokens
                dealt[pl.ds(pl.multiple_of(row, 8), tokens), :] = both[
                    k * tokens : (k + 1) * tokens
                ]

        done += count * rows

    size = share * tokens
    for r, ref in enumerate((own_ref, near_ref, over_ref, far_ref)):
        ref[...] = dealt[r * size : (r + 1) * size, :]


def project(cands, act, grad, win, wout, tokens, groups, ways, slots, padded):
    examples = cands.shape[1]
    rows = act.shape[0]
    pieces = 8
    step = rows // pieces
    blocks = ((2, step), (3, 2 * step))
    share = rows // ways
    hbm = pl.BlockSpec(memory_space=pltpu.HBM)
    vmem = pl.BlockSpec(memory_space=pltpu.VMEM)
    return pl.pallas_call(
        functools.partial(project_kernel, groups, ways, tokens, slots, padded, blocks),
        in_specs=[hbm] * 5,
        out_specs=[vmem] * 4 + [pl.BlockSpec(memory_space=pltpu.SMEM)] * 2,
        out_shape=[pltpu.VMEM((share, LANES), jnp.float32)] * 4
        + [
            pltpu.SMEM((examples,), jnp.int32),
            jax.ShapeDtypeStruct((1, examples), jnp.int32),
        ],
        scratch_shapes=[
            pltpu.VMEM(act.shape, jnp.bfloat16),
            pltpu.VMEM(grad.shape, jnp.bfloat16),
            pltpu.VMEM(win.shape, jnp.bfloat16),
            pltpu.VMEM(wout.shape, jnp.bfloat16),
            pltpu.VMEM(wout.shape, jnp.bfloat16),
            pltpu.VMEM((rows, LANES), jnp.float32),
            pltpu.SMEM((1, examples), jnp.int32),
            pltpu.SMEM((examples,), jnp.int32),
            pltpu.SMEM((groups,), jnp.int32),
            pltpu.SemaphoreType.DMA((pieces,)),
            pltpu.SemaphoreType.DMA((pieces,)),
            pltpu.SemaphoreType.DMA((3,)),
        ],
        compiler_params=pltpu.CompilerParams(vmem_limit_bytes=61 << 20),
        cost_estimate=pl.CostEstimate(
            flops=2 * rows * (act.shape[1] + grad.shape[1]) * 64,
            bytes_accessed=2 * rows * (act.shape[1] + grad.shape[1]),
            transcendentals=0,
        ),
        name="project",
    )(cands, act, grad, win, wout)


def own_kernel(slot_ref, a_ref, b_ref, q_hbm, out_slot_ref, out_ref, held_ref, sems):
    parts, _, width = held_ref.shape

    def load(k):
        columns = q_hbm.at[:, pl.ds(k * width, width)]
        return pltpu.make_async_copy(columns, held_ref.at[k], sems.at[k])

    for k in range(parts):
        load(k).start()
    out_ref[...] = a_ref[...] + b_ref[...]

    @pl.loop(0, out_slot_ref.shape[0])
    def _(i):
        out_slot_ref[i] = slot_ref[i]

    for k in range(parts):
        load(k).wait()


def own_sum(slots, a, b, queries, count, parts):
    smem = pl.BlockSpec(memory_space=pltpu.SMEM)
    vmem = pl.BlockSpec(memory_space=pltpu.VMEM)
    return pl.pallas_call(
        own_kernel,
        in_specs=[smem, vmem, vmem, pl.BlockSpec(memory_space=pltpu.HBM)],
        out_specs=[smem, vmem, vmem],
        out_shape=[
            pltpu.SMEM((count,), jnp.int32),
            pltpu.VMEM(a.shape, a.dtype),
            pltpu.VMEM((parts, queries.shape[0], queries.shape[1] // parts), queries.dtype),
        ],
        scratch_shapes=[pltpu.SemaphoreType.DMA((parts,))],
        compiler_params=pltpu.CompilerParams(vmem_limit_bytes=48 << 20),
        cost_estimate=pl.CostEstimate(
            flops=a.size, bytes_accessed=2 * queries.size, transcendentals=0
        ),
        name="own_sum",
    )(slots, a, b, queries)


def unit_kernel(tokens, chunks, row_ref, a_ref, b_ref, *rest):
    out_refs, total, units = rest[:-2], rest[-2], rest[-1]
    total[...] = a_ref[...] + b_ref[...]
    units[...] = jnp.zeros_like(units)
    count = total.shape[0] // tokens
    half = LANES // 2
    width = chunks * LANES
    low = lax.broadcasted_iota(jnp.int32, (chunks, LANES), 1) < half
    low_t = lax.broadcasted_iota(jnp.int32, (tokens, LANES), 1) < half

    @pl.loop(0, count, unroll=16)
    def _(i):
        part = total[pl.ds(pl.multiple_of(i * tokens, 8), tokens), :]
        twice = jnp.where(low_t, pltpu.roll(part, half, 1), part)
        g_hi = part.astype(jnp.bfloat16).astype(jnp.float32)
        a_hi = twice.astype(jnp.bfloat16).astype(jnp.float32)
        left = jnp.concatenate([g_hi, g_hi, part - g_hi], axis=0)[:, :half].astype(jnp.bfloat16)
        right = jnp.concatenate([a_hi, twice - a_hi, a_hi], axis=0).astype(jnp.bfloat16)
        prod = lax.dot_general(left, right, TN, preferred_element_type=jnp.float32)
        entries = jnp.where(low, prod[:chunks], prod[chunks : 2 * chunks])
        square = jnp.sum(entries * entries, axis=0, keepdims=True)
        mean = jnp.sum(square, axis=1, keepdims=True) / width
        unit = (entries * lax.rsqrt(mean + epsilon)).astype(jnp.bfloat16)
        row = pl.multiple_of(row_ref[i] * chunks, chunks)
        units[pl.ds(row, chunks), :] = unit

    for n, ref in enumerate(out_refs):
        size = ref.shape[0]
        ref[...] = units[n * size : (n + 1) * size, :]


def unit_grads(slots, a, b, tokens, chunks, groups, slot_count):
    rows = slot_count * chunks
    whole = pl.BlockSpec(memory_space=pltpu.VMEM)
    return pl.pallas_call(
        functools.partial(unit_kernel, tokens, chunks),
        in_specs=[pl.BlockSpec(memory_space=pltpu.SMEM), whole, whole],
        out_specs=[whole] * groups,
        out_shape=[pltpu.VMEM((rows, LANES), jnp.bfloat16)] * groups,
        scratch_shapes=[
            pltpu.VMEM(a.shape, jnp.float32),
            pltpu.VMEM((groups * rows, LANES), jnp.bfloat16),
        ],
        compiler_params=pltpu.CompilerParams(vmem_limit_bytes=16 << 20),
        cost_estimate=pl.CostEstimate(flops=20_000_000, bytes_accessed=1_000_000, transcendentals=0),
        name="unit_grads",
    )(slots, a, b)


def stage_units(refs, parcels, stage, parts, slots, groups):
    each = stage.shape[1] // (len(refs) // len(parcels) * groups * slots)
    span = slots * parts * each
    home = lax.axis_index("dp")
    for n, ref in enumerate(refs):
        parcel = parcels[n % len(parcels)]

        @pl.loop(0, len(parcel))
        def _(i, n=n, ref=ref, parcel=parcel):
            d = (parcel.start + parcel.step * i) ^ home
            got = ref[pl.ds(pl.multiple_of(i * span, span), span), :].astype(jnp.float32)
            got = got.reshape(slots, parts, each, LANES)
            for k in range(parts):
                at = pl.multiple_of((n // len(parcels) * groups + d) * slots * each, each)
                stage[k, pl.ds(at, slots * each), :] = got[:, k].reshape(slots * each, LANES)


def staged_rows(stage, k, units, at):
    rows = units.shape[0] - at
    each = units.shape[1] // LANES
    for j in range(each):
        piece = stage[k, pl.ds(j, rows, stride=each), :]
        units[at:, j * LANES : (j + 1) * LANES] = piece.astype(jnp.bfloat16)


def stage_kernel(groups, slots, parcels, *rest):
    refs, (out_ref, stage) = rest[:-2], rest[-2:]
    parts = out_ref.shape[0]
    stage_units(refs, parcels, stage, parts, slots, groups)

    @pl.loop(0, parts)
    def _(k):
        staged_rows(stage, k, out_ref.at[k], 0)


def staged(units, parcels, groups, slots, parts):
    rows = 2 * groups * slots
    width = sum(x.size for x in units) // (rows * parts)
    vmem = pl.BlockSpec(memory_space=pltpu.VMEM)
    return pl.pallas_call(
        functools.partial(stage_kernel, groups, slots, parcels),
        in_specs=[vmem] * len(units),
        out_specs=vmem,
        out_shape=pltpu.VMEM((parts, rows, width), jnp.bfloat16),
        scratch_shapes=[pltpu.VMEM((parts, rows * width // LANES, LANES), jnp.float32)],
        compiler_params=pltpu.CompilerParams(vmem_limit_bytes=16 << 20),
        cost_estimate=pl.CostEstimate(
            flops=rows * parts * width, bytes_accessed=8 * rows * width, transcendentals=0
        ),
        name="staged",
    )(*units)


def score_kernel(groups, slots, padded, parcels, *rest):
    refs, (early_ref, q_ref, out_ref, stage, units, total) = rest[:-6], rest[-6:]
    parts = q_ref.shape[0]
    half = groups * slots
    stage_units(refs, parcels, stage, parts, slots, groups)
    total[...] = jnp.zeros_like(total)

    @pl.loop(0, parts)
    def _(k):
        units[0 : 2 * half, :] = early_ref[k]
        staged_rows(stage, k, units, 2 * half)
        total[...] += lax.dot_general(q_ref[k], units[...], NT, preferred_element_type=jnp.float32)

    row = lax.broadcasted_iota(jnp.int32, (groups * padded, 4 * half), 0)
    column = lax.broadcasted_iota(jnp.int32, (1, 4 * half), 1)
    place = column
    for n in range(1, 4):
        place += jnp.where(column >= n * half, slots - half, 0)
    for n in range(4):
        for d in range(1, groups):
            after = (column >= n * half + d * slots) & (column < (n + 1) * half)
            place += jnp.where(after, padded - slots, 0)
    pick = jnp.where(row == place, 1.0, 0.0).astype(jnp.bfloat16)
    out = lax.dot_general(
        pick, total[...].astype(jnp.bfloat16), NT, preferred_element_type=jnp.float32
    )
    out_ref[...] = out.astype(out_ref.dtype)


def scores_of(late, early, queries, parcels, groups, slots, padded):
    parts, count, width = queries.shape
    half = groups * slots
    vmem = pl.BlockSpec(memory_space=pltpu.VMEM)
    return pl.pallas_call(
        functools.partial(score_kernel, groups, slots, padded, parcels),
        in_specs=[vmem] * (len(late) + 2),
        out_specs=vmem,
        out_shape=pltpu.VMEM((groups * padded, count), jnp.bfloat16),
        scratch_shapes=[
            pltpu.VMEM((parts, 2 * half * width // LANES, LANES), jnp.float32),
            pltpu.VMEM((4 * half, width), jnp.bfloat16),
            pltpu.VMEM((count, 4 * half), jnp.float32),
        ],
        compiler_params=pltpu.CompilerParams(vmem_limit_bytes=24 << 20),
        cost_estimate=pl.CostEstimate(
            flops=2 * 4 * half * queries.size, bytes_accessed=2 * queries.size, transcendentals=0
        ),
        name="scores",
    )(*late, early, queries)


def pick_kernel(row_ref, x_ref, out_ref):
    count = row_ref.shape[1]
    rows = x_ref.shape[0]
    parts = x_ref.shape[1] // LANES
    hit = lax.broadcasted_iota(jnp.int32, (rows, count), 0) == row_ref[...]
    pick = jnp.where(hit, 1.0, 0.0).T.astype(jnp.bfloat16)
    got = jnp.dot(pick, x_ref[...], preferred_element_type=jnp.float32)
    for j in range(parts):
        out_ref[pl.ds(j, count, stride=parts), :] = got[:, j * LANES : (j + 1) * LANES]


def pick_rows(row, x):
    vmem = pl.BlockSpec(memory_space=pltpu.VMEM)
    count, width = row.shape[1], x.shape[1]
    return pl.pallas_call(
        pick_kernel,
        in_specs=[vmem, vmem],
        out_specs=vmem,
        out_shape=jax.ShapeDtypeStruct((count * (width // LANES), LANES), jnp.float32),
        compiler_params=pltpu.CompilerParams(vmem_limit_bytes=16 << 20),
        cost_estimate=pl.CostEstimate(flops=16_000_000, bytes_accessed=400_000, transcendentals=0),
        name="pick_rows",
    )(row, x)


def local_one(activations, out_grads, proj_in, proj_out, queries, candidates):
    examples, tokens, hidden = activations.shape
    features = out_grads.shape[2]
    groups = lax.axis_size("dp")
    ways = lax.axis_size("tensor")
    capacity = max(2, 5 * examples // (2 * groups))
    slots = -(-capacity // ways)
    padded = -(-ways * slots // 8) * 8
    query_block = queries[0]
    chunks = query_block.shape[1] // LANES
    core = [(i, i ^ 1) for i in range(ways)]
    across = [(i, i ^ 2) for i in range(ways)]

    own_part, over_part, near_part, far_part, my_slots, pick = project(
        candidates.reshape(1, examples),
        activations.reshape(examples * tokens, hidden),
        out_grads.reshape(examples * tokens, features),
        proj_in.T,
        proj_out.T,
        tokens,
        groups,
        ways,
        slots,
        padded,
    )
    far_in = lax.ppermute(far_part, "tensor", core)
    near_in = lax.ppermute(near_part, "tensor", core)
    across_in = lax.ppermute(over_part + far_in, "tensor", across)

    here_slots, here, held = own_sum(
        my_slots, own_part, near_in, query_block, examples // ways, 1
    )
    units = unit_grads(here_slots, here, across_in, tokens, chunks, groups, slots)
    parcels = (range(0, groups, 2), range(1, groups, 2))
    arrived = [units[0]] + [None] * (groups - 1)
    farthest = groups - 1
    for k in (farthest, *range(groups - 2, 0, -2), *range(groups - 3, 0, -2)):
        block = units[k]
        if k % 2 and k < groups // 2:
            block, _ = lax.optimization_barrier((block, arrived[farthest]))
        arrived[k] = lax.ppermute(block, "dp", [(i, i ^ k) for i in range(groups)])
    own = [jnp.concatenate([arrived[k] for k in parcel], axis=0) for parcel in parcels]
    over_y = [lax.ppermute(x, "tensor", across) for x in own]
    over_core = [lax.ppermute(x, "tensor", core) for x in own]
    early = staged(own + over_core, parcels, groups, slots, held.shape[0])
    over_both = [lax.ppermute(x, "tensor", core) for x in over_y]
    both = scores_of(over_y + over_both, early, held, parcels, groups, slots, padded)
    block = both.reshape(groups, padded, both.shape[1])
    returned = lax.all_to_all(block, "dp", split_axis=0, concat_axis=0, tiled=True)
    picked = pick_rows(pick, returned.reshape(both.shape))
    return picked.reshape(examples, 1, both.shape[1])


def local_many(activations, out_grads, proj_in, proj_out, queries, candidates):
    examples_here, tokens_here, hidden_here = activations.shape
    proj_rank = proj_in.shape[1]
    per_example = candidates.shape[1]
    groups = lax.axis_size("dp")
    capacity = max(2, 5 * examples_here * per_example // (2 * groups))
    act_proj = jnp.dot(
        activations.reshape(examples_here * tokens_here, hidden_here),
        proj_in,
        preferred_element_type=jnp.float32,
    )
    grad_proj = jnp.dot(
        out_grads.reshape(examples_here * tokens_here, out_grads.shape[2]),
        proj_out,
        preferred_element_type=jnp.float32,
    )
    both_proj = jnp.concatenate([grad_proj, act_proj], axis=1).reshape(
        examples_here, tokens_here, 2 * proj_rank
    )
    summed = lax.psum(both_proj, "tensor")
    grad_side = summed[:, :, :proj_rank]
    act_side = summed[:, :, proj_rank:]
    example_grads = jnp.einsum(
        "eta,etb->eab", grad_side, act_side, precision=lax.Precision.HIGHEST
    ).reshape(examples_here, proj_rank * proj_rank)
    inv_rms = lax.rsqrt(jnp.mean(example_grads * example_grads, axis=1, keepdims=True) + epsilon)
    unit = (example_grads * inv_rms).astype(jnp.bfloat16)
    flat_cands = candidates.reshape(-1)
    hit_table = (flat_cands[:, None] == jnp.arange(groups, dtype=jnp.int32)[None, :]).astype(
        jnp.int32
    )
    earlier = jnp.cumsum(hit_table, axis=0) - hit_table
    slot_index = jnp.sum(earlier * hit_table, axis=1)
    dest_index = flat_cands * capacity + slot_index
    row_copies = jnp.repeat(unit, per_example, axis=0)
    grad_width = unit.shape[1]
    send_buffer = (
        jnp.zeros((groups * capacity, grad_width), jnp.bfloat16).at[dest_index].set(row_copies)
    )
    send_buffer = send_buffer.reshape(groups, capacity, grad_width)
    col_width = grad_width // lax.axis_size("tensor")
    column_part = lax.dynamic_slice_in_dim(
        send_buffer, lax.axis_index("tensor") * col_width, col_width, 2
    )
    received = lax.all_to_all(column_part, "dp", split_axis=0, concat_axis=0, tiled=True)
    slot_scores = jnp.einsum(
        "gsk,qk->gsq",
        lax.all_gather(received, "tensor", axis=2, tiled=True),
        queries[0],
        preferred_element_type=jnp.float32,
    )
    returned = lax.all_to_all(slot_scores, "dp", split_axis=0, concat_axis=0, tiled=True)
    picked = returned.reshape(groups * capacity, returned.shape[2])[dest_index]
    return picked.reshape(examples_here, per_example, returned.shape[2])


def local(activations, out_grads, proj_in, proj_out, queries, candidates):
    groups = lax.axis_size("dp")
    one = candidates.shape[1] == 1 and lax.axis_size("tensor") == 4
    one = one and groups >= 4 and groups & (groups - 1) == 0
    return (local_one if one else local_many)(
        activations, out_grads, proj_in, proj_out, queries, candidates
    )


def solution(mesh):
    placed = (
        P("dp", None, "tensor"),
        P("dp", None, "tensor"),
        P("tensor", None),
        P("tensor", None),
        P("dp", "tensor", None),
        P("dp", None),
    )
    return jax.shard_map(
        local, mesh=mesh, in_specs=placed, out_specs=P("dp", None, "tensor"), check_vma=False
    )
```

```python
import functools

import jax
import jax.numpy as jnp
from jax import lax
from jax.experimental import pallas as pl
from jax.experimental.pallas import tpu as pltpu
from jax.sharding import PartitionSpec as P

epsilon = 1e-06
LANES = 128
NT = (((1,), (1,)), ((), ()))
TN = (((0,), (0,)), ((), ()))

PLANS = {8: (((0, 6, 5, 7, 3), (1, 2, 4)), {1: 5, 2: 7})}


def project_kernel(
    groups, ways, tokens, slots, padded, blocks,
    cand_hbm, act_hbm, grad_hbm, win_hbm, wout_hbm,
    own_ref, over_ref, near_ref, far_ref, slot_ref, pick_ref,
    act, grad, win, wout, raw, dealt, cand, rank, start, act_sems, grad_sems, sems,
):
    proj_rank = win.shape[0]
    examples = cand.shape[1]
    share = examples // ways
    step = act.shape[0] // act_sems.shape[0]
    me = lax.axis_index("tensor")
    home = lax.axis_index("dp")

    def piece(i):
        return pl.ds(pl.multiple_of(i * step, step), step)

    def act_copy(i):
        return pltpu.make_async_copy(act_hbm.at[piece(i)], act.at[piece(i)], act_sems.at[i])

    def grad_copy(i):
        return pltpu.make_async_copy(grad_hbm.at[piece(i)], grad.at[piece(i)], grad_sems.at[i])

    cand_copy = pltpu.make_async_copy(cand_hbm, cand, sems.at[0])
    raw_copy = pltpu.make_async_copy(wout_hbm, raw, sems.at[1])
    win_copy = pltpu.make_async_copy(win_hbm, win, sems.at[2])
    cand_copy.start()
    raw_copy.start()
    win_copy.start()

    @pl.loop(0, act_sems.shape[0])
    def _(i):
        act_copy(i).start()
        grad_copy(i).start()

    cand_copy.wait()

    @pl.loop(0, groups)
    def _(g):
        start[g] = 0

    @pl.loop(0, examples)
    def _(e):
        g = cand[0, e]
        rank[e] = start[g]
        start[g] = start[g] + 1

    def shift(g, below):
        here = start[g]
        start[g] = below
        return below + here

    lax.fori_loop(0, groups, shift, jnp.int32(0))

    half = proj_rank // 2
    r = lax.broadcasted_iota(jnp.int32, (proj_rank, proj_rank), 0)
    c = lax.broadcasted_iota(jnp.int32, (proj_rank, proj_rank), 1)
    pick = (c == jnp.where(r < half, 2 * r, 2 * (r - half) + 1)).astype(jnp.bfloat16)
    raw_copy.wait()
    wout[...] = jnp.dot(pick, raw[...], preferred_element_type=jnp.float32).astype(jnp.bfloat16)
    win_copy.wait()

    done = 0
    for count, rows in blocks:

        @pl.loop(0, count)
        def _(i, done=done, rows=rows):
            for j in range(rows // step):
                act_copy(done // step + i * (rows // step) + j).wait()
                grad_copy(done // step + i * (rows // step) + j).wait()
            at = pl.multiple_of(done + i * rows, step)
            here = pl.ds(at, rows)
            left = lax.dot_general(grad[here, :], wout[...], NT, preferred_element_type=jnp.float32)
            right = lax.dot_general(act[here, :], win[...], NT, preferred_element_type=jnp.float32)
            both = jnp.concatenate([left, right], axis=1)
            first = done // tokens + i * (rows // tokens)
            for k in range(rows // tokens):
                e = first + k
                g = cand[0, e]
                place = start[g] + rank[e]
                owner = place & (ways - 1)
                turn = place >> (ways.bit_length() - 1)
                before = (start[g] + ways - 1 - owner) >> (ways.bit_length() - 1)
                rel = owner ^ me
                slot_ref[rel * share + turn] = (g ^ home) * slots + turn - before
                pick_ref[0, e] = g * padded + rel * slots + turn - before
                row = (rel * share + turn) * tokens
                dealt[pl.ds(pl.multiple_of(row, 8), tokens), :] = both[
                    k * tokens : (k + 1) * tokens
                ]

        done += count * rows

    size = share * tokens
    for r, ref in enumerate((own_ref, near_ref, over_ref, far_ref)):
        ref[...] = dealt[r * size : (r + 1) * size, :]


def project(cands, act, grad, win, wout, tokens, groups, ways, slots, padded):
    examples = cands.shape[1]
    rows = act.shape[0]
    pieces = 8
    step = rows // pieces
    blocks = ((2, step), (3, 2 * step))
    share = rows // ways
    hbm = pl.BlockSpec(memory_space=pltpu.HBM)
    vmem = pl.BlockSpec(memory_space=pltpu.VMEM)
    return pl.pallas_call(
        functools.partial(project_kernel, groups, ways, tokens, slots, padded, blocks),
        in_specs=[hbm] * 5,
        out_specs=[vmem] * 4 + [pl.BlockSpec(memory_space=pltpu.SMEM)] * 2,
        out_shape=[pltpu.VMEM((share, LANES), jnp.float32)] * 4
        + [
            pltpu.SMEM((examples,), jnp.int32),
            jax.ShapeDtypeStruct((1, examples), jnp.int32),
        ],
        scratch_shapes=[
            pltpu.VMEM(act.shape, jnp.bfloat16),
            pltpu.VMEM(grad.shape, jnp.bfloat16),
            pltpu.VMEM(win.shape, jnp.bfloat16),
            pltpu.VMEM(wout.shape, jnp.bfloat16),
            pltpu.VMEM(wout.shape, jnp.bfloat16),
            pltpu.VMEM((rows, LANES), jnp.float32),
            pltpu.SMEM((1, examples), jnp.int32),
            pltpu.SMEM((examples,), jnp.int32),
            pltpu.SMEM((groups,), jnp.int32),
            pltpu.SemaphoreType.DMA((pieces,)),
            pltpu.SemaphoreType.DMA((pieces,)),
            pltpu.SemaphoreType.DMA((3,)),
        ],
        compiler_params=pltpu.CompilerParams(vmem_limit_bytes=61 << 20),
        cost_estimate=pl.CostEstimate(
            flops=2 * rows * (act.shape[1] + grad.shape[1]) * 64,
            bytes_accessed=2 * rows * (act.shape[1] + grad.shape[1]),
            transcendentals=0,
        ),
        name="project",
    )(cands, act, grad, win, wout)


def own_kernel(slot_ref, a_ref, b_ref, q_hbm, out_slot_ref, out_ref, held_ref, sems):
    parts = sems.shape[0]
    rows = held_ref.shape[0] // parts

    def load(k):
        here = pl.ds(k * rows, rows)
        return pltpu.make_async_copy(q_hbm.at[here], held_ref.at[here], sems.at[k])

    for k in range(parts):
        load(k).start()
    out_ref[...] = a_ref[...] + b_ref[...]

    @pl.loop(0, out_slot_ref.shape[0])
    def _(i):
        out_slot_ref[i] = slot_ref[i]

    for k in range(parts):
        load(k).wait()


def own_sum(slots, a, b, queries, count):
    smem = pl.BlockSpec(memory_space=pltpu.SMEM)
    vmem = pl.BlockSpec(memory_space=pltpu.VMEM)
    parts = 4 if queries.shape[0] % 64 == 0 else 1
    return pl.pallas_call(
        own_kernel,
        in_specs=[smem, vmem, vmem, pl.BlockSpec(memory_space=pltpu.HBM)],
        out_specs=[smem, vmem, vmem],
        out_shape=[
            pltpu.SMEM((count,), jnp.int32),
            pltpu.VMEM(a.shape, a.dtype),
            pltpu.VMEM(queries.shape, queries.dtype),
        ],
        scratch_shapes=[pltpu.SemaphoreType.DMA((parts,))],
        compiler_params=pltpu.CompilerParams(vmem_limit_bytes=48 << 20),
        cost_estimate=pl.CostEstimate(
            flops=a.size, bytes_accessed=2 * queries.size, transcendentals=0
        ),
        name="own_sum",
    )(slots, a, b, queries)


def unit_kernel(tokens, chunks, row_ref, a_ref, b_ref, *rest):
    out_refs, total, units = rest[:-2], rest[-2], rest[-1]
    total[...] = a_ref[...] + b_ref[...]
    units[...] = jnp.zeros_like(units)
    count = total.shape[0] // tokens
    half = LANES // 2
    width = chunks * LANES
    low = lax.broadcasted_iota(jnp.int32, (chunks, LANES), 1) < half
    low_t = lax.broadcasted_iota(jnp.int32, (tokens, LANES), 1) < half

    @pl.loop(0, count, unroll=16)
    def _(i):
        part = total[pl.ds(pl.multiple_of(i * tokens, 8), tokens), :]
        twice = jnp.where(low_t, pltpu.roll(part, half, 1), part)
        g_hi = part.astype(jnp.bfloat16).astype(jnp.float32)
        a_hi = twice.astype(jnp.bfloat16).astype(jnp.float32)
        left = jnp.concatenate([g_hi, g_hi, part - g_hi], axis=0)[:, :half].astype(jnp.bfloat16)
        right = jnp.concatenate([a_hi, twice - a_hi, a_hi], axis=0).astype(jnp.bfloat16)
        prod = lax.dot_general(left, right, TN, preferred_element_type=jnp.float32)
        entries = jnp.where(low, prod[:chunks], prod[chunks : 2 * chunks])
        square = jnp.sum(entries * entries, axis=0, keepdims=True)
        mean = jnp.sum(square, axis=1, keepdims=True) / width
        unit = (entries * lax.rsqrt(mean + epsilon)).astype(jnp.bfloat16)
        row = pl.multiple_of(row_ref[i] * chunks, chunks)
        units[pl.ds(row, chunks), :] = unit

    for n, ref in enumerate(out_refs):
        size = ref.shape[0]
        ref[...] = units[n * size : (n + 1) * size, :]


def unit_grads(slots, a, b, tokens, chunks, groups, slot_count):
    rows = slot_count * chunks
    whole = pl.BlockSpec(memory_space=pltpu.VMEM)
    return pl.pallas_call(
        functools.partial(unit_kernel, tokens, chunks),
        in_specs=[pl.BlockSpec(memory_space=pltpu.SMEM), whole, whole],
        out_specs=[whole] * groups,
        out_shape=[pltpu.VMEM((rows, LANES), jnp.bfloat16)] * groups,
        scratch_shapes=[
            pltpu.VMEM(a.shape, jnp.float32),
            pltpu.VMEM((groups * rows, LANES), jnp.bfloat16),
        ],
        compiler_params=pltpu.CompilerParams(vmem_limit_bytes=16 << 20),
        cost_estimate=pl.CostEstimate(flops=20_000_000, bytes_accessed=1_000_000, transcendentals=0),
        name="unit_grads",
    )(slots, a, b)


def stage_units(refs, parcels, stage, groups):
    span = stage.shape[0] // (len(refs) // len(parcels) * groups)
    home = lax.axis_index("dp")
    for n, ref in enumerate(refs):
        for i, distance in enumerate(parcels[n % len(parcels)]):
            block = n // len(parcels) * groups + (distance ^ home)
            here = pl.ds(pl.multiple_of(block * span, span), span)
            stage[here, :] = ref[i * span : (i + 1) * span, :].astype(jnp.float32)


def staged_rows(stage, units, at):
    rows = units.shape[0] - at
    chunks = units.shape[1] // LANES
    for j in range(chunks):
        piece = stage[pl.ds(j, rows, stride=chunks), :]
        units[at:, j * LANES : (j + 1) * LANES] = piece.astype(jnp.bfloat16)


def stage_kernel(groups, parcels, *rest):
    refs, (out_ref, stage) = rest[:-2], rest[-2:]
    stage_units(refs, parcels, stage, groups)
    staged_rows(stage, out_ref, 0)


def staged(units, parcels, groups, slots):
    rows = 2 * groups * slots
    width = sum(x.size for x in units) // rows
    vmem = pl.BlockSpec(memory_space=pltpu.VMEM)
    return pl.pallas_call(
        functools.partial(stage_kernel, groups, parcels),
        in_specs=[vmem] * len(units),
        out_specs=vmem,
        out_shape=pltpu.VMEM((rows, width), jnp.bfloat16),
        scratch_shapes=[pltpu.VMEM((rows * width // LANES, LANES), jnp.float32)],
        compiler_params=pltpu.CompilerParams(vmem_limit_bytes=16 << 20),
        cost_estimate=pl.CostEstimate(
            flops=rows * width, bytes_accessed=8 * rows * width, transcendentals=0
        ),
        name="staged",
    )(*units)


def score_kernel(groups, slots, padded, parcels, *rest):
    refs, (early_ref, q_ref, out_ref, stage, units) = rest[:-5], rest[-5:]
    half = groups * slots
    stage_units(refs, parcels, stage, groups)
    units[0 : 2 * half, :] = early_ref[...]
    staged_rows(stage, units, 2 * half)
    total = lax.dot_general(q_ref[...], units[...], NT, preferred_element_type=jnp.float32)

    row = lax.broadcasted_iota(jnp.int32, (groups * padded, 4 * half), 0)
    column = lax.broadcasted_iota(jnp.int32, (1, 4 * half), 1)
    place = column
    for n in range(1, 4):
        place += jnp.where(column >= n * half, slots - half, 0)
    for n in range(4):
        for d in range(1, groups):
            after = (column >= n * half + d * slots) & (column < (n + 1) * half)
            place += jnp.where(after, padded - slots, 0)
    pick = jnp.where(row == place, 1.0, 0.0).astype(jnp.bfloat16)
    out = lax.dot_general(
        pick, total.astype(jnp.bfloat16), NT, preferred_element_type=jnp.float32
    )
    out_ref[...] = out.astype(out_ref.dtype)


def scores_of(late, early, queries, parcels, groups, slots, padded):
    count, width = queries.shape
    half = groups * slots
    vmem = pl.BlockSpec(memory_space=pltpu.VMEM)
    return pl.pallas_call(
        functools.partial(score_kernel, groups, slots, padded, parcels),
        in_specs=[vmem] * (len(late) + 2),
        out_specs=vmem,
        out_shape=pltpu.VMEM((groups * padded, count), jnp.bfloat16),
        scratch_shapes=[
            pltpu.VMEM((2 * half * width // LANES, LANES), jnp.float32),
            pltpu.VMEM((4 * half, width), jnp.bfloat16),
        ],
        compiler_params=pltpu.CompilerParams(vmem_limit_bytes=24 << 20),
        cost_estimate=pl.CostEstimate(
            flops=2 * 4 * half * queries.size, bytes_accessed=2 * queries.size, transcendentals=0
        ),
        name="scores",
    )(*late, early, queries)


def pick_kernel(row_ref, x_ref, out_ref):
    count = row_ref.shape[1]
    rows = x_ref.shape[0]
    parts = x_ref.shape[1] // LANES
    hit = lax.broadcasted_iota(jnp.int32, (rows, count), 0) == row_ref[...]
    pick = jnp.where(hit, 1.0, 0.0).T.astype(jnp.bfloat16)
    got = jnp.dot(pick, x_ref[...], preferred_element_type=jnp.float32)
    for j in range(parts):
        out_ref[pl.ds(j, count, stride=parts), :] = got[:, j * LANES : (j + 1) * LANES]


def pick_rows(row, x):
    vmem = pl.BlockSpec(memory_space=pltpu.VMEM)
    count, width = row.shape[1], x.shape[1]
    return pl.pallas_call(
        pick_kernel,
        in_specs=[vmem, vmem],
        out_specs=vmem,
        out_shape=jax.ShapeDtypeStruct((count * (width // LANES), LANES), jnp.float32),
        compiler_params=pltpu.CompilerParams(vmem_limit_bytes=16 << 20),
        cost_estimate=pl.CostEstimate(flops=16_000_000, bytes_accessed=400_000, transcendentals=0),
        name="pick_rows",
    )(row, x)


def local_one(activations, out_grads, proj_in, proj_out, queries, candidates):
    examples, tokens, hidden = activations.shape
    features = out_grads.shape[2]
    groups = lax.axis_size("dp")
    ways = lax.axis_size("tensor")
    capacity = max(2, 5 * examples // (2 * groups))
    slots = -(-capacity // ways)
    padded = -(-ways * slots // 8) * 8
    query_block = queries[0]
    chunks = query_block.shape[1] // LANES
    core = [(i, i ^ 1) for i in range(ways)]
    across = [(i, i ^ 2) for i in range(ways)]

    own_part, over_part, near_part, far_part, my_slots, pick = project(
        candidates.reshape(1, examples),
        activations.reshape(examples * tokens, hidden),
        out_grads.reshape(examples * tokens, features),
        proj_in.T,
        proj_out.T,
        tokens,
        groups,
        ways,
        slots,
        padded,
    )
    far_in = lax.ppermute(far_part, "tensor", core)
    near_in = lax.ppermute(near_part, "tensor", core)
    across_in = lax.ppermute(over_part + far_in, "tensor", across)

    here_slots, here, held = own_sum(
        my_slots, own_part, near_in, query_block, examples // ways
    )
    units = unit_grads(here_slots, here, across_in, tokens, chunks, groups, slots)
    parcels, after = PLANS[groups]
    arrived = [units[0]] + [None] * (groups - 1)
    for k in (k for parcel in parcels for k in parcel if k):
        block = units[k]
        if k in after:
            block, _ = lax.optimization_barrier((block, arrived[after[k]]))
        arrived[k] = lax.ppermute(block, "dp", [(i, i ^ k) for i in range(groups)])
    own = [jnp.concatenate([arrived[k] for k in parcel], axis=0) for parcel in parcels]
    over_y = [lax.ppermute(x, "tensor", across) for x in own]
    over_core = [lax.ppermute(x, "tensor", core) for x in own]
    early = staged(own + over_core, parcels, groups, slots)
    over_both = [lax.ppermute(x, "tensor", core) for x in over_y]
    both = scores_of(over_y + over_both, early, held, parcels, groups, slots, padded)
    block = both.reshape(groups, padded, both.shape[1])
    returned = lax.all_to_all(block, "dp", split_axis=0, concat_axis=0, tiled=True)
    picked = pick_rows(pick, returned.reshape(both.shape))
    return picked.reshape(examples, 1, both.shape[1])


def local_many(activations, out_grads, proj_in, proj_out, queries, candidates):
    examples_here, tokens_here, hidden_here = activations.shape
    proj_rank = proj_in.shape[1]
    per_example = candidates.shape[1]
    groups = lax.axis_size("dp")
    capacity = max(2, 5 * examples_here * per_example // (2 * groups))
    act_proj = jnp.dot(
        activations.reshape(examples_here * tokens_here, hidden_here),
        proj_in,
        preferred_element_type=jnp.float32,
    )
    grad_proj = jnp.dot(
        out_grads.reshape(examples_here * tokens_here, out_grads.shape[2]),
        proj_out,
        preferred_element_type=jnp.float32,
    )
    both_proj = jnp.concatenate([grad_proj, act_proj], axis=1).reshape(
        examples_here, tokens_here, 2 * proj_rank
    )
    summed = lax.psum(both_proj, "tensor")
    grad_side = summed[:, :, :proj_rank]
    act_side = summed[:, :, proj_rank:]
    example_grads = jnp.einsum(
        "eta,etb->eab", grad_side, act_side, precision=lax.Precision.HIGHEST
    ).reshape(examples_here, proj_rank * proj_rank)
    inv_rms = lax.rsqrt(jnp.mean(example_grads * example_grads, axis=1, keepdims=True) + epsilon)
    unit = (example_grads * inv_rms).astype(jnp.bfloat16)
    flat_cands = candidates.reshape(-1)
    hit_table = (flat_cands[:, None] == jnp.arange(groups, dtype=jnp.int32)[None, :]).astype(
        jnp.int32
    )
    earlier = jnp.cumsum(hit_table, axis=0) - hit_table
    slot_index = jnp.sum(earlier * hit_table, axis=1)
    dest_index = flat_cands * capacity + slot_index
    row_copies = jnp.repeat(unit, per_example, axis=0)
    grad_width = unit.shape[1]
    send_buffer = (
        jnp.zeros((groups * capacity, grad_width), jnp.bfloat16).at[dest_index].set(row_copies)
    )
    send_buffer = send_buffer.reshape(groups, capacity, grad_width)
    col_width = grad_width // lax.axis_size("tensor")
    column_part = lax.dynamic_slice_in_dim(
        send_buffer, lax.axis_index("tensor") * col_width, col_width, 2
    )
    received = lax.all_to_all(column_part, "dp", split_axis=0, concat_axis=0, tiled=True)
    slot_scores = jnp.einsum(
        "gsk,qk->gsq",
        lax.all_gather(received, "tensor", axis=2, tiled=True),
        queries[0],
        preferred_element_type=jnp.float32,
    )
    returned = lax.all_to_all(slot_scores, "dp", split_axis=0, concat_axis=0, tiled=True)
    picked = returned.reshape(groups * capacity, returned.shape[2])[dest_index]
    return picked.reshape(examples_here, per_example, returned.shape[2])


def local(activations, out_grads, proj_in, proj_out, queries, candidates):
    one = candidates.shape[1] == 1 and lax.axis_size("tensor") == 4
    one = one and lax.axis_size("dp") in PLANS
    return (local_one if one else local_many)(
        activations, out_grads, proj_in, proj_out, queries, candidates
    )


def solution(mesh):
    placed = (
        P("dp", None, "tensor"),
        P("dp", None, "tensor"),
        P("tensor", None),
        P("tensor", None),
        P("dp", "tensor", None),
        P("dp", None),
    )
    return jax.shard_map(
        local, mesh=mesh, in_specs=placed, out_specs=P("dp", None, "tensor"), check_vma=False
    )
```

```python
import functools

import jax
import jax.numpy as jnp
from jax import lax
from jax.experimental import pallas as pl
from jax.experimental.pallas import tpu as pltpu
from jax.sharding import PartitionSpec as P

epsilon = 1e-06
LANES = 128
NT = (((1,), (1,)), ((), ()))
TN = (((0,), (0,)), ((), ()))

PLANS = {8: (((0, 6, 5, 7, 3), (1, 2, 4)), {1: 5, 2: 7})}


def project_kernel(
    groups, ways, tokens, slots, padded, blocks,
    cand_hbm, act_hbm, grad_hbm, win_hbm, wout_hbm,
    own_ref, over_ref, near_ref, far_ref, slot_ref, pick_ref,
    x, w, raw, dealt, cand, rank, start, act_sems, grad_sems, sems,
):
    proj_rank = win_hbm.shape[0]
    features = grad_hbm.shape[1]
    total = x.shape[1]
    examples = cand.shape[1]
    share = examples // ways
    step = x.shape[0] // act_sems.shape[0]
    me = lax.axis_index("tensor")
    home = lax.axis_index("dp")

    def piece(i):
        return pl.ds(pl.multiple_of(i * step, step), step)

    def act_copy(i):
        there = x.at[piece(i), pl.ds(features, total - features)]
        return pltpu.make_async_copy(act_hbm.at[piece(i)], there, act_sems.at[i])

    def grad_copy(i):
        there = x.at[piece(i), pl.ds(0, features)]
        return pltpu.make_async_copy(grad_hbm.at[piece(i)], there, grad_sems.at[i])

    cand_copy = pltpu.make_async_copy(cand_hbm, cand, sems.at[0])
    raw_copy = pltpu.make_async_copy(wout_hbm, raw, sems.at[1])
    there = w.at[pl.ds(proj_rank, proj_rank), pl.ds(features, total - features)]
    win_copy = pltpu.make_async_copy(win_hbm, there, sems.at[2])
    cand_copy.start()
    raw_copy.start()
    win_copy.start()

    @pl.loop(0, act_sems.shape[0])
    def _(i):
        act_copy(i).start()
        grad_copy(i).start()

    cand_copy.wait()

    @pl.loop(0, groups)
    def _(g):
        start[g] = 0

    @pl.loop(0, examples)
    def _(e):
        g = cand[0, e]
        rank[e] = start[g]
        start[g] = start[g] + 1

    def shift(g, below):
        here = start[g]
        start[g] = below
        return below + here

    lax.fori_loop(0, groups, shift, jnp.int32(0))

    half = proj_rank // 2
    r = lax.broadcasted_iota(jnp.int32, (proj_rank, proj_rank), 0)
    c = lax.broadcasted_iota(jnp.int32, (proj_rank, proj_rank), 1)
    pick = (c == jnp.where(r < half, 2 * r, 2 * (r - half) + 1)).astype(jnp.bfloat16)
    raw_copy.wait()
    w[0:proj_rank, 0:features] = jnp.dot(
        pick, raw[...], preferred_element_type=jnp.float32
    ).astype(jnp.bfloat16)
    w[proj_rank:, 0:features] = jnp.zeros((proj_rank, features), w.dtype)
    w[0:proj_rank, features:] = jnp.zeros((proj_rank, total - features), w.dtype)
    win_copy.wait()

    done = 0
    for count, rows in blocks:

        @pl.loop(0, count)
        def _(i, done=done, rows=rows):
            for j in range(rows // step):
                act_copy(done // step + i * (rows // step) + j).wait()
                grad_copy(done // step + i * (rows // step) + j).wait()
            at = pl.multiple_of(done + i * rows, step)
            here = pl.ds(at, rows)
            both = lax.dot_general(x[here, :], w[...], NT, preferred_element_type=jnp.float32)
            first = done // tokens + i * (rows // tokens)
            for k in range(rows // tokens):
                e = first + k
                g = cand[0, e]
                place = start[g] + rank[e]
                owner = place & (ways - 1)
                turn = place >> (ways.bit_length() - 1)
                before = (start[g] + ways - 1 - owner) >> (ways.bit_length() - 1)
                rel = owner ^ me
                slot_ref[rel * share + turn] = (g ^ home) * slots + turn - before
                pick_ref[0, e] = g * padded + rel * slots + turn - before
                row = (rel * share + turn) * tokens
                dealt[pl.ds(pl.multiple_of(row, 8), tokens), :] = both[
                    k * tokens : (k + 1) * tokens
                ]

        done += count * rows

    size = share * tokens
    for r, ref in enumerate((own_ref, near_ref, over_ref, far_ref)):
        ref[...] = dealt[r * size : (r + 1) * size, :]


def project(cands, act, grad, win, wout, tokens, groups, ways, slots, padded):
    examples = cands.shape[1]
    rows = act.shape[0]
    pieces = 8
    step = rows // pieces
    blocks = ((2, step), (3, 2 * step))
    share = rows // ways
    hbm = pl.BlockSpec(memory_space=pltpu.HBM)
    vmem = pl.BlockSpec(memory_space=pltpu.VMEM)
    return pl.pallas_call(
        functools.partial(project_kernel, groups, ways, tokens, slots, padded, blocks),
        in_specs=[hbm] * 5,
        out_specs=[vmem] * 4 + [pl.BlockSpec(memory_space=pltpu.SMEM)] * 2,
        out_shape=[pltpu.VMEM((share, LANES), jnp.float32)] * 4
        + [
            pltpu.SMEM((examples,), jnp.int32),
            jax.ShapeDtypeStruct((1, examples), jnp.int32),
        ],
        scratch_shapes=[
            pltpu.VMEM((rows, act.shape[1] + grad.shape[1]), jnp.bfloat16),
            pltpu.VMEM((2 * win.shape[0], act.shape[1] + grad.shape[1]), jnp.bfloat16),
            pltpu.VMEM(wout.shape, jnp.bfloat16),
            pltpu.VMEM((rows, LANES), jnp.float32),
            pltpu.SMEM((1, examples), jnp.int32),
            pltpu.SMEM((examples,), jnp.int32),
            pltpu.SMEM((groups,), jnp.int32),
            pltpu.SemaphoreType.DMA((pieces,)),
            pltpu.SemaphoreType.DMA((pieces,)),
            pltpu.SemaphoreType.DMA((3,)),
        ],
        compiler_params=pltpu.CompilerParams(vmem_limit_bytes=61 << 20),
        cost_estimate=pl.CostEstimate(
            flops=2 * rows * (act.shape[1] + grad.shape[1]) * 64,
            bytes_accessed=2 * rows * (act.shape[1] + grad.shape[1]),
            transcendentals=0,
        ),
        name="project",
    )(cands, act, grad, win, wout)


def own_kernel(slot_ref, a_ref, b_ref, q_hbm, out_slot_ref, out_ref, held_ref, sems):
    parts = sems.shape[0]
    rows = held_ref.shape[0] // parts

    def load(k):
        here = pl.ds(k * rows, rows)
        return pltpu.make_async_copy(q_hbm.at[here], held_ref.at[here], sems.at[k])

    for k in range(parts):
        load(k).start()
    out_ref[...] = a_ref[...] + b_ref[...]

    @pl.loop(0, out_slot_ref.shape[0])
    def _(i):
        out_slot_ref[i] = slot_ref[i]

    for k in range(parts):
        load(k).wait()


def own_sum(slots, a, b, queries, count):
    smem = pl.BlockSpec(memory_space=pltpu.SMEM)
    vmem = pl.BlockSpec(memory_space=pltpu.VMEM)
    parts = 4 if queries.shape[0] % 64 == 0 else 1
    return pl.pallas_call(
        own_kernel,
        in_specs=[smem, vmem, vmem, pl.BlockSpec(memory_space=pltpu.HBM)],
        out_specs=[smem, vmem, vmem],
        out_shape=[
            pltpu.SMEM((count,), jnp.int32),
            pltpu.VMEM(a.shape, a.dtype),
            pltpu.VMEM(queries.shape, queries.dtype),
        ],
        scratch_shapes=[pltpu.SemaphoreType.DMA((parts,))],
        compiler_params=pltpu.CompilerParams(vmem_limit_bytes=48 << 20),
        cost_estimate=pl.CostEstimate(
            flops=a.size, bytes_accessed=2 * queries.size, transcendentals=0
        ),
        name="own_sum",
    )(slots, a, b, queries)


def unit_kernel(tokens, chunks, row_ref, a_ref, b_ref, *rest):
    out_refs, total, units = rest[:-2], rest[-2], rest[-1]
    total[...] = a_ref[...] + b_ref[...]
    units[...] = jnp.zeros_like(units)
    count = total.shape[0] // tokens
    half = LANES // 2
    width = chunks * LANES
    low = lax.broadcasted_iota(jnp.int32, (chunks, LANES), 1) < half
    low_t = lax.broadcasted_iota(jnp.int32, (tokens, LANES), 1) < half

    @pl.loop(0, count, unroll=16)
    def _(i):
        part = total[pl.ds(pl.multiple_of(i * tokens, 8), tokens), :]
        twice = jnp.where(low_t, pltpu.roll(part, half, 1), part)
        g_hi = part.astype(jnp.bfloat16).astype(jnp.float32)
        a_hi = twice.astype(jnp.bfloat16).astype(jnp.float32)
        left = jnp.concatenate([g_hi, g_hi, part - g_hi], axis=0)[:, :half].astype(jnp.bfloat16)
        right = jnp.concatenate([a_hi, twice - a_hi, a_hi], axis=0).astype(jnp.bfloat16)
        prod = lax.dot_general(left, right, TN, preferred_element_type=jnp.float32)
        entries = jnp.where(low, prod[:chunks], prod[chunks : 2 * chunks])
        square = jnp.sum(entries * entries, axis=0, keepdims=True)
        mean = jnp.sum(square, axis=1, keepdims=True) / width
        unit = (entries * lax.rsqrt(mean + epsilon)).astype(jnp.bfloat16)
        row = pl.multiple_of(row_ref[i] * chunks, chunks)
        units[pl.ds(row, chunks), :] = unit

    for n, ref in enumerate(out_refs):
        size = ref.shape[0]
        ref[...] = units[n * size : (n + 1) * size, :]


def unit_grads(slots, a, b, tokens, chunks, groups, slot_count):
    rows = slot_count * chunks
    whole = pl.BlockSpec(memory_space=pltpu.VMEM)
    return pl.pallas_call(
        functools.partial(unit_kernel, tokens, chunks),
        in_specs=[pl.BlockSpec(memory_space=pltpu.SMEM), whole, whole],
        out_specs=[whole] * groups,
        out_shape=[pltpu.VMEM((rows, LANES), jnp.bfloat16)] * groups,
        scratch_shapes=[
            pltpu.VMEM(a.shape, jnp.float32),
            pltpu.VMEM((groups * rows, LANES), jnp.bfloat16),
        ],
        compiler_params=pltpu.CompilerParams(vmem_limit_bytes=16 << 20),
        cost_estimate=pl.CostEstimate(flops=20_000_000, bytes_accessed=1_000_000, transcendentals=0),
        name="unit_grads",
    )(slots, a, b)


def stage_units(refs, parcels, stage, groups):
    span = stage.shape[0] // (len(refs) // len(parcels) * groups)
    home = lax.axis_index("dp")
    for n, ref in enumerate(refs):
        for i, distance in enumerate(parcels[n % len(parcels)]):
            block = n // len(parcels) * groups + (distance ^ home)
            here = pl.ds(pl.multiple_of(block * span, span), span)
            stage[here, :] = ref[i * span : (i + 1) * span, :].astype(jnp.float32)


def staged_rows(stage, units, at):
    rows = units.shape[0] - at
    chunks = units.shape[1] // LANES
    for j in range(chunks):
        piece = stage[pl.ds(j, rows, stride=chunks), :]
        units[at:, j * LANES : (j + 1) * LANES] = piece.astype(jnp.bfloat16)


def stage_kernel(groups, parcels, *rest):
    refs, (out_ref, stage) = rest[:-2], rest[-2:]
    stage_units(refs, parcels, stage, groups)
    staged_rows(stage, out_ref, 0)


def staged(units, parcels, groups, slots):
    rows = 2 * groups * slots
    width = sum(x.size for x in units) // rows
    vmem = pl.BlockSpec(memory_space=pltpu.VMEM)
    return pl.pallas_call(
        functools.partial(stage_kernel, groups, parcels),
        in_specs=[vmem] * len(units),
        out_specs=vmem,
        out_shape=pltpu.VMEM((rows, width), jnp.bfloat16),
        scratch_shapes=[pltpu.VMEM((rows * width // LANES, LANES), jnp.float32)],
        compiler_params=pltpu.CompilerParams(vmem_limit_bytes=16 << 20),
        cost_estimate=pl.CostEstimate(
            flops=rows * width, bytes_accessed=8 * rows * width, transcendentals=0
        ),
        name="staged",
    )(*units)


def score_kernel(groups, slots, padded, parcels, *rest):
    refs, (early_ref, q_ref, out_ref, stage, units) = rest[:-5], rest[-5:]
    half = groups * slots
    stage_units(refs, parcels, stage, groups)
    units[0 : 2 * half, :] = early_ref[...]
    staged_rows(stage, units, 2 * half)
    total = lax.dot_general(q_ref[...], units[...], NT, preferred_element_type=jnp.float32)

    row = lax.broadcasted_iota(jnp.int32, (groups * padded, 4 * half), 0)
    column = lax.broadcasted_iota(jnp.int32, (1, 4 * half), 1)
    place = column
    for n in range(1, 4):
        place += jnp.where(column >= n * half, slots - half, 0)
    for n in range(4):
        for d in range(1, groups):
            after = (column >= n * half + d * slots) & (column < (n + 1) * half)
            place += jnp.where(after, padded - slots, 0)
    pick = jnp.where(row == place, 1.0, 0.0).astype(jnp.bfloat16)
    out = lax.dot_general(
        pick, total.astype(jnp.bfloat16), NT, preferred_element_type=jnp.float32
    )
    out_ref[...] = out.astype(out_ref.dtype)


def scores_of(late, early, queries, parcels, groups, slots, padded):
    count, width = queries.shape
    half = groups * slots
    vmem = pl.BlockSpec(memory_space=pltpu.VMEM)
    return pl.pallas_call(
        functools.partial(score_kernel, groups, slots, padded, parcels),
        in_specs=[vmem] * (len(late) + 2),
        out_specs=vmem,
        out_shape=pltpu.VMEM((groups * padded, count), jnp.bfloat16),
        scratch_shapes=[
            pltpu.VMEM((2 * half * width // LANES, LANES), jnp.float32),
            pltpu.VMEM((4 * half, width), jnp.bfloat16),
        ],
        compiler_params=pltpu.CompilerParams(vmem_limit_bytes=24 << 20),
        cost_estimate=pl.CostEstimate(
            flops=2 * 4 * half * queries.size, bytes_accessed=2 * queries.size, transcendentals=0
        ),
        name="scores",
    )(*late, early, queries)


def pick_kernel(row_ref, x_ref, out_ref):
    count = row_ref.shape[1]
    rows = x_ref.shape[0]
    parts = x_ref.shape[1] // LANES
    hit = lax.broadcasted_iota(jnp.int32, (rows, count), 0) == row_ref[...]
    pick = jnp.where(hit, 1.0, 0.0).T.astype(jnp.bfloat16)
    got = jnp.dot(pick, x_ref[...], preferred_element_type=jnp.float32)
    for j in range(parts):
        out_ref[pl.ds(j, count, stride=parts), :] = got[:, j * LANES : (j + 1) * LANES]


def pick_rows(row, x):
    vmem = pl.BlockSpec(memory_space=pltpu.VMEM)
    count, width = row.shape[1], x.shape[1]
    return pl.pallas_call(
        pick_kernel,
        in_specs=[vmem, vmem],
        out_specs=vmem,
        out_shape=jax.ShapeDtypeStruct((count * (width // LANES), LANES), jnp.float32),
        compiler_params=pltpu.CompilerParams(vmem_limit_bytes=16 << 20),
        cost_estimate=pl.CostEstimate(flops=16_000_000, bytes_accessed=400_000, transcendentals=0),
        name="pick_rows",
    )(row, x)


def local_one(activations, out_grads, proj_in, proj_out, queries, candidates):
    examples, tokens, hidden = activations.shape
    features = out_grads.shape[2]
    groups = lax.axis_size("dp")
    ways = lax.axis_size("tensor")
    capacity = max(2, 5 * examples // (2 * groups))
    slots = -(-capacity // ways)
    padded = -(-ways * slots // 8) * 8
    query_block = queries[0]
    chunks = query_block.shape[1] // LANES
    core = [(i, i ^ 1) for i in range(ways)]
    across = [(i, i ^ 2) for i in range(ways)]

    own_part, over_part, near_part, far_part, my_slots, pick = project(
        candidates.reshape(1, examples),
        activations.reshape(examples * tokens, hidden),
        out_grads.reshape(examples * tokens, features),
        proj_in.T,
        proj_out.T,
        tokens,
        groups,
        ways,
        slots,
        padded,
    )
    far_in = lax.ppermute(far_part, "tensor", core)
    near_in = lax.ppermute(near_part, "tensor", core)
    across_in = lax.ppermute(over_part + far_in, "tensor", across)

    here_slots, here, held = own_sum(
        my_slots, own_part, near_in, query_block, examples // ways
    )
    units = unit_grads(here_slots, here, across_in, tokens, chunks, groups, slots)
    parcels, after = PLANS[groups]
    arrived = [units[0]] + [None] * (groups - 1)
    for k in (k for parcel in parcels for k in parcel if k):
        block = units[k]
        if k in after:
            block, _ = lax.optimization_barrier((block, arrived[after[k]]))
        arrived[k] = lax.ppermute(block, "dp", [(i, i ^ k) for i in range(groups)])
    own = [jnp.concatenate([arrived[k] for k in parcel], axis=0) for parcel in parcels]
    over_y = [lax.ppermute(x, "tensor", across) for x in own]
    over_core = [lax.ppermute(x, "tensor", core) for x in own]
    early = staged(own + over_core, parcels, groups, slots)
    over_both = [lax.ppermute(x, "tensor", core) for x in over_y]
    both = scores_of(over_y + over_both, early, held, parcels, groups, slots, padded)
    block = both.reshape(groups, padded, both.shape[1])
    returned = lax.all_to_all(block, "dp", split_axis=0, concat_axis=0, tiled=True)
    picked = pick_rows(pick, returned.reshape(both.shape))
    return picked.reshape(examples, 1, both.shape[1])


def local_many(activations, out_grads, proj_in, proj_out, queries, candidates):
    examples_here, tokens_here, hidden_here = activations.shape
    proj_rank = proj_in.shape[1]
    per_example = candidates.shape[1]
    groups = lax.axis_size("dp")
    capacity = max(2, 5 * examples_here * per_example // (2 * groups))
    act_proj = jnp.dot(
        activations.reshape(examples_here * tokens_here, hidden_here),
        proj_in,
        preferred_element_type=jnp.float32,
    )
    grad_proj = jnp.dot(
        out_grads.reshape(examples_here * tokens_here, out_grads.shape[2]),
        proj_out,
        preferred_element_type=jnp.float32,
    )
    both_proj = jnp.concatenate([grad_proj, act_proj], axis=1).reshape(
        examples_here, tokens_here, 2 * proj_rank
    )
    summed = lax.psum(both_proj, "tensor")
    grad_side = summed[:, :, :proj_rank]
    act_side = summed[:, :, proj_rank:]
    example_grads = jnp.einsum(
        "eta,etb->eab", grad_side, act_side, precision=lax.Precision.HIGHEST
    ).reshape(examples_here, proj_rank * proj_rank)
    inv_rms = lax.rsqrt(jnp.mean(example_grads * example_grads, axis=1, keepdims=True) + epsilon)
    unit = (example_grads * inv_rms).astype(jnp.bfloat16)
    flat_cands = candidates.reshape(-1)
    hit_table = (flat_cands[:, None] == jnp.arange(groups, dtype=jnp.int32)[None, :]).astype(
        jnp.int32
    )
    earlier = jnp.cumsum(hit_table, axis=0) - hit_table
    slot_index = jnp.sum(earlier * hit_table, axis=1)
    dest_index = flat_cands * capacity + slot_index
    row_copies = jnp.repeat(unit, per_example, axis=0)
    grad_width = unit.shape[1]
    send_buffer = (
        jnp.zeros((groups * capacity, grad_width), jnp.bfloat16).at[dest_index].set(row_copies)
    )
    send_buffer = send_buffer.reshape(groups, capacity, grad_width)
    col_width = grad_width // lax.axis_size("tensor")
    column_part = lax.dynamic_slice_in_dim(
        send_buffer, lax.axis_index("tensor") * col_width, col_width, 2
    )
    received = lax.all_to_all(column_part, "dp", split_axis=0, concat_axis=0, tiled=True)
    slot_scores = jnp.einsum(
        "gsk,qk->gsq",
        lax.all_gather(received, "tensor", axis=2, tiled=True),
        queries[0],
        preferred_element_type=jnp.float32,
    )
    returned = lax.all_to_all(slot_scores, "dp", split_axis=0, concat_axis=0, tiled=True)
    picked = returned.reshape(groups * capacity, returned.shape[2])[dest_index]
    return picked.reshape(examples_here, per_example, returned.shape[2])


def local(activations, out_grads, proj_in, proj_out, queries, candidates):
    one = candidates.shape[1] == 1 and lax.axis_size("tensor") == 4
    one = one and lax.axis_size("dp") in PLANS
    return (local_one if one else local_many)(
        activations, out_grads, proj_in, proj_out, queries, candidates
    )


def solution(mesh):
    placed = (
        P("dp", None, "tensor"),
        P("dp", None, "tensor"),
        P("tensor", None),
        P("tensor", None),
        P("dp", "tensor", None),
        P("dp", None),
    )
    return jax.shard_map(
        local, mesh=mesh, in_specs=placed, out_specs=P("dp", None, "tensor"), check_vma=False
    )
```

```python
import functools

import jax
import jax.numpy as jnp
from jax import lax
from jax.experimental import pallas as pl
from jax.experimental.pallas import tpu as pltpu
from jax.sharding import PartitionSpec as P

epsilon = 1e-06
LANES = 128
NT = (((1,), (1,)), ((), ()))
TN = (((0,), (0,)), ((), ()))

PLANS = {8: (((0, 4, 7, 3, 6), (5, 1, 2)), {2: 4})}


def project_kernel(
    groups, ways, tokens, slots, padded, blocks,
    cand_hbm, act_hbm, grad_hbm, win_hbm, wout_hbm,
    own_ref, over_ref, near_ref, far_ref, slot_ref, pick_ref,
    x, w, raw, dealt, cand, rank, start, act_sems, grad_sems, sems,
):
    proj_rank = win_hbm.shape[0]
    features = grad_hbm.shape[1]
    total = x.shape[1]
    examples = cand.shape[1]
    share = examples // ways
    step = x.shape[0] // act_sems.shape[0]
    me = lax.axis_index("tensor")
    home = lax.axis_index("dp")

    def piece(i):
        return pl.ds(pl.multiple_of(i * step, step), step)

    def act_copy(i):
        there = x.at[piece(i), pl.ds(features, total - features)]
        return pltpu.make_async_copy(act_hbm.at[piece(i)], there, act_sems.at[i])

    def grad_copy(i):
        there = x.at[piece(i), pl.ds(0, features)]
        return pltpu.make_async_copy(grad_hbm.at[piece(i)], there, grad_sems.at[i])

    cand_copy = pltpu.make_async_copy(cand_hbm, cand, sems.at[0])
    raw_copy = pltpu.make_async_copy(wout_hbm, raw, sems.at[1])
    there = w.at[pl.ds(proj_rank, proj_rank), pl.ds(features, total - features)]
    win_copy = pltpu.make_async_copy(win_hbm, there, sems.at[2])
    cand_copy.start()
    raw_copy.start()
    win_copy.start()

    @pl.loop(0, act_sems.shape[0])
    def _(i):
        act_copy(i).start()
        grad_copy(i).start()

    cand_copy.wait()

    @pl.loop(0, groups)
    def _(g):
        start[g] = 0

    @pl.loop(0, examples)
    def _(e):
        g = cand[0, e]
        rank[e] = start[g]
        start[g] = start[g] + 1

    def shift(g, below):
        here = start[g]
        start[g] = below
        return below + here

    lax.fori_loop(0, groups, shift, jnp.int32(0))

    half = proj_rank // 2
    r = lax.broadcasted_iota(jnp.int32, (proj_rank, proj_rank), 0)
    c = lax.broadcasted_iota(jnp.int32, (proj_rank, proj_rank), 1)
    pick = (c == jnp.where(r < half, 2 * r, 2 * (r - half) + 1)).astype(jnp.bfloat16)
    raw_copy.wait()
    w[0:proj_rank, 0:features] = jnp.dot(
        pick, raw[...], preferred_element_type=jnp.float32
    ).astype(jnp.bfloat16)
    w[proj_rank:, 0:features] = jnp.zeros((proj_rank, features), w.dtype)
    w[0:proj_rank, features:] = jnp.zeros((proj_rank, total - features), w.dtype)
    win_copy.wait()

    done = 0
    for count, rows in blocks:

        @pl.loop(0, count)
        def _(i, done=done, rows=rows):
            for j in range(rows // step):
                act_copy(done // step + i * (rows // step) + j).wait()
                grad_copy(done // step + i * (rows // step) + j).wait()
            at = pl.multiple_of(done + i * rows, step)
            here = pl.ds(at, rows)
            both = lax.dot_general(x[here, :], w[...], NT, preferred_element_type=jnp.float32)
            first = done // tokens + i * (rows // tokens)
            for k in range(rows // tokens):
                e = first + k
                g = cand[0, e]
                place = start[g] + rank[e]
                owner = place & (ways - 1)
                turn = place >> (ways.bit_length() - 1)
                before = (start[g] + ways - 1 - owner) >> (ways.bit_length() - 1)
                rel = owner ^ me
                slot_ref[rel * share + turn] = (g ^ home) * slots + turn - before
                pick_ref[0, e] = g * padded + rel * slots + turn - before
                row = (rel * share + turn) * tokens
                dealt[pl.ds(pl.multiple_of(row, 8), tokens), :] = both[
                    k * tokens : (k + 1) * tokens
                ]

        done += count * rows

    size = share * tokens
    for r, ref in enumerate((own_ref, near_ref, over_ref, far_ref)):
        ref[...] = dealt[r * size : (r + 1) * size, :]


def project(cands, act, grad, win, wout, tokens, groups, ways, slots, padded):
    examples = cands.shape[1]
    rows = act.shape[0]
    pieces = 8
    step = rows // pieces
    blocks = ((2, step), (3, 2 * step))
    share = rows // ways
    hbm = pl.BlockSpec(memory_space=pltpu.HBM)
    vmem = pl.BlockSpec(memory_space=pltpu.VMEM)
    return pl.pallas_call(
        functools.partial(project_kernel, groups, ways, tokens, slots, padded, blocks),
        in_specs=[hbm] * 5,
        out_specs=[vmem] * 4 + [pl.BlockSpec(memory_space=pltpu.SMEM)] * 2,
        out_shape=[pltpu.VMEM((share, LANES), jnp.float32)] * 4
        + [
            pltpu.SMEM((examples,), jnp.int32),
            jax.ShapeDtypeStruct((1, examples), jnp.int32),
        ],
        scratch_shapes=[
            pltpu.VMEM((rows, act.shape[1] + grad.shape[1]), jnp.bfloat16),
            pltpu.VMEM((2 * win.shape[0], act.shape[1] + grad.shape[1]), jnp.bfloat16),
            pltpu.VMEM(wout.shape, jnp.bfloat16),
            pltpu.VMEM((rows, LANES), jnp.float32),
            pltpu.SMEM((1, examples), jnp.int32),
            pltpu.SMEM((examples,), jnp.int32),
            pltpu.SMEM((groups,), jnp.int32),
            pltpu.SemaphoreType.DMA((pieces,)),
            pltpu.SemaphoreType.DMA((pieces,)),
            pltpu.SemaphoreType.DMA((3,)),
        ],
        compiler_params=pltpu.CompilerParams(vmem_limit_bytes=61 << 20),
        cost_estimate=pl.CostEstimate(
            flops=2 * rows * (act.shape[1] + grad.shape[1]) * 64,
            bytes_accessed=2 * rows * (act.shape[1] + grad.shape[1]),
            transcendentals=0,
        ),
        name="project",
    )(cands, act, grad, win, wout)


def own_kernel(slot_ref, a_ref, b_ref, q_hbm, out_slot_ref, out_ref, held_ref, sems):
    parts = sems.shape[0]
    rows = held_ref.shape[0] // parts

    def load(k):
        here = pl.ds(k * rows, rows)
        return pltpu.make_async_copy(q_hbm.at[here], held_ref.at[here], sems.at[k])

    for k in range(parts):
        load(k).start()
    out_ref[...] = a_ref[...] + b_ref[...]

    @pl.loop(0, out_slot_ref.shape[0])
    def _(i):
        out_slot_ref[i] = slot_ref[i]

    for k in range(parts):
        load(k).wait()


def own_sum(slots, a, b, queries, count):
    smem = pl.BlockSpec(memory_space=pltpu.SMEM)
    vmem = pl.BlockSpec(memory_space=pltpu.VMEM)
    parts = 4 if queries.shape[0] % 64 == 0 else 1
    return pl.pallas_call(
        own_kernel,
        in_specs=[smem, vmem, vmem, pl.BlockSpec(memory_space=pltpu.HBM)],
        out_specs=[smem, vmem, vmem],
        out_shape=[
            pltpu.SMEM((count,), jnp.int32),
            pltpu.VMEM(a.shape, a.dtype),
            pltpu.VMEM(queries.shape, queries.dtype),
        ],
        scratch_shapes=[pltpu.SemaphoreType.DMA((parts,))],
        compiler_params=pltpu.CompilerParams(vmem_limit_bytes=48 << 20),
        cost_estimate=pl.CostEstimate(
            flops=a.size, bytes_accessed=2 * queries.size, transcendentals=0
        ),
        name="own_sum",
    )(slots, a, b, queries)


def unit_kernel(tokens, chunks, row_ref, a_ref, b_ref, *rest):
    out_refs, total, units = rest[:-2], rest[-2], rest[-1]
    total[...] = a_ref[...] + b_ref[...]
    units[...] = jnp.zeros_like(units)
    count = total.shape[0] // tokens
    half = LANES // 2
    width = chunks * LANES
    low = lax.broadcasted_iota(jnp.int32, (chunks, LANES), 1) < half
    low_t = lax.broadcasted_iota(jnp.int32, (tokens, LANES), 1) < half

    @pl.loop(0, count, unroll=16)
    def _(i):
        part = total[pl.ds(pl.multiple_of(i * tokens, 8), tokens), :]
        twice = jnp.where(low_t, pltpu.roll(part, half, 1), part)
        g_hi = part.astype(jnp.bfloat16).astype(jnp.float32)
        a_hi = twice.astype(jnp.bfloat16).astype(jnp.float32)
        left = jnp.concatenate([g_hi, g_hi, part - g_hi], axis=0)[:, :half].astype(jnp.bfloat16)
        right = jnp.concatenate([a_hi, twice - a_hi, a_hi], axis=0).astype(jnp.bfloat16)
        prod = lax.dot_general(left, right, TN, preferred_element_type=jnp.float32)
        entries = jnp.where(low, prod[:chunks], prod[chunks : 2 * chunks])
        square = jnp.sum(entries * entries, axis=0, keepdims=True)
        mean = jnp.sum(square, axis=1, keepdims=True) / width
        unit = (entries * lax.rsqrt(mean + epsilon)).astype(jnp.bfloat16)
        row = pl.multiple_of(row_ref[i] * chunks, chunks)
        units[pl.ds(row, chunks), :] = unit

    for n, ref in enumerate(out_refs):
        size = ref.shape[0]
        ref[...] = units[n * size : (n + 1) * size, :]


def unit_grads(slots, a, b, tokens, chunks, groups, slot_count):
    rows = slot_count * chunks
    whole = pl.BlockSpec(memory_space=pltpu.VMEM)
    return pl.pallas_call(
        functools.partial(unit_kernel, tokens, chunks),
        in_specs=[pl.BlockSpec(memory_space=pltpu.SMEM), whole, whole],
        out_specs=[whole] * groups,
        out_shape=[pltpu.VMEM((rows, LANES), jnp.bfloat16)] * groups,
        scratch_shapes=[
            pltpu.VMEM(a.shape, jnp.float32),
            pltpu.VMEM((groups * rows, LANES), jnp.bfloat16),
        ],
        compiler_params=pltpu.CompilerParams(vmem_limit_bytes=16 << 20),
        cost_estimate=pl.CostEstimate(flops=20_000_000, bytes_accessed=1_000_000, transcendentals=0),
        name="unit_grads",
    )(slots, a, b)


def stage_units(refs, parcels, stage, groups):
    span = stage.shape[0] // (len(refs) // len(parcels) * groups)
    home = lax.axis_index("dp")
    for n, ref in enumerate(refs):
        for i, distance in enumerate(parcels[n % len(parcels)]):
            block = n // len(parcels) * groups + (distance ^ home)
            here = pl.ds(pl.multiple_of(block * span, span), span)
            stage[here, :] = ref[i * span : (i + 1) * span, :].astype(jnp.float32)


def staged_rows(stage, units, at):
    rows = units.shape[0] - at
    chunks = units.shape[1] // LANES
    for j in range(chunks):
        piece = stage[pl.ds(j, rows, stride=chunks), :]
        units[at:, j * LANES : (j + 1) * LANES] = piece.astype(jnp.bfloat16)


def stage_kernel(groups, parcels, *rest):
    refs, (out_ref, stage) = rest[:-2], rest[-2:]
    stage_units(refs, parcels, stage, groups)
    staged_rows(stage, out_ref, 0)


def staged(units, parcels, groups, slots):
    rows = 2 * groups * slots
    width = sum(x.size for x in units) // rows
    vmem = pl.BlockSpec(memory_space=pltpu.VMEM)
    return pl.pallas_call(
        functools.partial(stage_kernel, groups, parcels),
        in_specs=[vmem] * len(units),
        out_specs=vmem,
        out_shape=pltpu.VMEM((rows, width), jnp.bfloat16),
        scratch_shapes=[pltpu.VMEM((rows * width // LANES, LANES), jnp.float32)],
        compiler_params=pltpu.CompilerParams(vmem_limit_bytes=16 << 20),
        cost_estimate=pl.CostEstimate(
            flops=rows * width, bytes_accessed=8 * rows * width, transcendentals=0
        ),
        name="staged",
    )(*units)


def score_kernel(groups, slots, padded, parcels, *rest):
    refs, (early_ref, q_ref, out_ref, stage, units) = rest[:-5], rest[-5:]
    half = groups * slots
    stage_units(refs, parcels, stage, groups)
    units[0 : 2 * half, :] = early_ref[...]
    staged_rows(stage, units, 2 * half)
    total = lax.dot_general(q_ref[...], units[...], NT, preferred_element_type=jnp.float32)

    row = lax.broadcasted_iota(jnp.int32, (groups * padded, 4 * half), 0)
    column = lax.broadcasted_iota(jnp.int32, (1, 4 * half), 1)
    place = column
    for n in range(1, 4):
        place += jnp.where(column >= n * half, slots - half, 0)
    for n in range(4):
        for d in range(1, groups):
            after = (column >= n * half + d * slots) & (column < (n + 1) * half)
            place += jnp.where(after, padded - slots, 0)
    pick = jnp.where(row == place, 1.0, 0.0).astype(jnp.bfloat16)
    out = lax.dot_general(
        pick, total.astype(jnp.bfloat16), NT, preferred_element_type=jnp.float32
    )
    out_ref[...] = out.astype(out_ref.dtype)


def scores_of(late, early, queries, parcels, groups, slots, padded):
    count, width = queries.shape
    half = groups * slots
    vmem = pl.BlockSpec(memory_space=pltpu.VMEM)
    return pl.pallas_call(
        functools.partial(score_kernel, groups, slots, padded, parcels),
        in_specs=[vmem] * (len(late) + 2),
        out_specs=vmem,
        out_shape=pltpu.VMEM((groups * padded, count), jnp.bfloat16),
        scratch_shapes=[
            pltpu.VMEM((2 * half * width // LANES, LANES), jnp.float32),
            pltpu.VMEM((4 * half, width), jnp.bfloat16),
        ],
        compiler_params=pltpu.CompilerParams(vmem_limit_bytes=24 << 20),
        cost_estimate=pl.CostEstimate(
            flops=2 * 4 * half * queries.size, bytes_accessed=2 * queries.size, transcendentals=0
        ),
        name="scores",
    )(*late, early, queries)


def pick_kernel(row_ref, x_ref, out_ref):
    count = row_ref.shape[1]
    rows = x_ref.shape[0]
    parts = x_ref.shape[1] // LANES
    hit = lax.broadcasted_iota(jnp.int32, (rows, count), 0) == row_ref[...]
    pick = jnp.where(hit, 1.0, 0.0).T.astype(jnp.bfloat16)
    got = jnp.dot(pick, x_ref[...], preferred_element_type=jnp.float32)
    for j in range(parts):
        out_ref[pl.ds(j, count, stride=parts), :] = got[:, j * LANES : (j + 1) * LANES]


def pick_rows(row, x):
    vmem = pl.BlockSpec(memory_space=pltpu.VMEM)
    count, width = row.shape[1], x.shape[1]
    return pl.pallas_call(
        pick_kernel,
        in_specs=[vmem, vmem],
        out_specs=vmem,
        out_shape=jax.ShapeDtypeStruct((count * (width // LANES), LANES), jnp.float32),
        compiler_params=pltpu.CompilerParams(vmem_limit_bytes=16 << 20),
        cost_estimate=pl.CostEstimate(flops=16_000_000, bytes_accessed=400_000, transcendentals=0),
        name="pick_rows",
    )(row, x)


def local_one(activations, out_grads, proj_in, proj_out, queries, candidates):
    examples, tokens, hidden = activations.shape
    features = out_grads.shape[2]
    groups = lax.axis_size("dp")
    ways = lax.axis_size("tensor")
    capacity = max(2, 5 * examples // (2 * groups))
    slots = -(-capacity // ways)
    padded = -(-ways * slots // 8) * 8
    query_block = queries[0]
    chunks = query_block.shape[1] // LANES
    core = [(i, i ^ 1) for i in range(ways)]
    across = [(i, i ^ 2) for i in range(ways)]

    own_part, over_part, near_part, far_part, my_slots, pick = project(
        candidates.reshape(1, examples),
        activations.reshape(examples * tokens, hidden),
        out_grads.reshape(examples * tokens, features),
        proj_in.T,
        proj_out.T,
        tokens,
        groups,
        ways,
        slots,
        padded,
    )
    far_in = lax.ppermute(far_part, "tensor", core)
    near_in = lax.ppermute(near_part, "tensor", core)
    across_in = lax.ppermute(over_part + far_in, "tensor", across)

    here_slots, here, held = own_sum(
        my_slots, own_part, near_in, query_block, examples // ways
    )
    units = unit_grads(here_slots, here, across_in, tokens, chunks, groups, slots)
    parcels, after = PLANS[groups]
    arrived = [units[0]] + [None] * (groups - 1)
    for k in (k for parcel in parcels for k in parcel if k):
        block = units[k]
        if k in after:
            block, _ = lax.optimization_barrier((block, arrived[after[k]]))
        arrived[k] = lax.ppermute(block, "dp", [(i, i ^ k) for i in range(groups)])
    own = [jnp.concatenate([arrived[k] for k in parcel], axis=0) for parcel in parcels]
    over_y = [lax.ppermute(x, "tensor", across) for x in own]
    over_core = [lax.ppermute(x, "tensor", core) for x in own]
    early = staged(own + over_core, parcels, groups, slots)
    over_both = [lax.ppermute(x, "tensor", core) for x in over_y]
    both = scores_of(over_y + over_both, early, held, parcels, groups, slots, padded)
    block = both.reshape(groups, padded, both.shape[1])
    returned = lax.all_to_all(block, "dp", split_axis=0, concat_axis=0, tiled=True)
    picked = pick_rows(pick, returned.reshape(both.shape))
    return picked.reshape(examples, 1, both.shape[1])


def local_many(activations, out_grads, proj_in, proj_out, queries, candidates):
    examples_here, tokens_here, hidden_here = activations.shape
    proj_rank = proj_in.shape[1]
    per_example = candidates.shape[1]
    groups = lax.axis_size("dp")
    capacity = max(2, 5 * examples_here * per_example // (2 * groups))
    act_proj = jnp.dot(
        activations.reshape(examples_here * tokens_here, hidden_here),
        proj_in,
        preferred_element_type=jnp.float32,
    )
    grad_proj = jnp.dot(
        out_grads.reshape(examples_here * tokens_here, out_grads.shape[2]),
        proj_out,
        preferred_element_type=jnp.float32,
    )
    both_proj = jnp.concatenate([grad_proj, act_proj], axis=1).reshape(
        examples_here, tokens_here, 2 * proj_rank
    )
    summed = lax.psum(both_proj, "tensor")
    grad_side = summed[:, :, :proj_rank]
    act_side = summed[:, :, proj_rank:]
    example_grads = jnp.einsum(
        "eta,etb->eab", grad_side, act_side, precision=lax.Precision.HIGHEST
    ).reshape(examples_here, proj_rank * proj_rank)
    inv_rms = lax.rsqrt(jnp.mean(example_grads * example_grads, axis=1, keepdims=True) + epsilon)
    unit = (example_grads * inv_rms).astype(jnp.bfloat16)
    flat_cands = candidates.reshape(-1)
    hit_table = (flat_cands[:, None] == jnp.arange(groups, dtype=jnp.int32)[None, :]).astype(
        jnp.int32
    )
    earlier = jnp.cumsum(hit_table, axis=0) - hit_table
    slot_index = jnp.sum(earlier * hit_table, axis=1)
    dest_index = flat_cands * capacity + slot_index
    row_copies = jnp.repeat(unit, per_example, axis=0)
    grad_width = unit.shape[1]
    send_buffer = (
        jnp.zeros((groups * capacity, grad_width), jnp.bfloat16).at[dest_index].set(row_copies)
    )
    send_buffer = send_buffer.reshape(groups, capacity, grad_width)
    col_width = grad_width // lax.axis_size("tensor")
    column_part = lax.dynamic_slice_in_dim(
        send_buffer, lax.axis_index("tensor") * col_width, col_width, 2
    )
    received = lax.all_to_all(column_part, "dp", split_axis=0, concat_axis=0, tiled=True)
    slot_scores = jnp.einsum(
        "gsk,qk->gsq",
        lax.all_gather(received, "tensor", axis=2, tiled=True),
        queries[0],
        preferred_element_type=jnp.float32,
    )
    returned = lax.all_to_all(slot_scores, "dp", split_axis=0, concat_axis=0, tiled=True)
    picked = returned.reshape(groups * capacity, returned.shape[2])[dest_index]
    return picked.reshape(examples_here, per_example, returned.shape[2])


def local(activations, out_grads, proj_in, proj_out, queries, candidates):
    one = candidates.shape[1] == 1 and lax.axis_size("tensor") == 4
    one = one and lax.axis_size("dp") in PLANS
    return (local_one if one else local_many)(
        activations, out_grads, proj_in, proj_out, queries, candidates
    )


def solution(mesh):
    placed = (
        P("dp", None, "tensor"),
        P("dp", None, "tensor"),
        P("tensor", None),
        P("tensor", None),
        P("dp", "tensor", None),
        P("dp", None),
    )
    return jax.shard_map(
        local, mesh=mesh, in_specs=placed, out_specs=P("dp", None, "tensor"), check_vma=False
    )
```

```python
import functools

import jax
import jax.numpy as jnp
from jax import lax
from jax.experimental import pallas as pl
from jax.experimental.pallas import tpu as pltpu
from jax.sharding import PartitionSpec as P

epsilon = 1e-06
LANES = 128
NT = (((1,), (1,)), ((), ()))
TN = (((0,), (0,)), ((), ()))

PLANS = {8: (((0, 4, 7, 3, 6), (5, 1, 2)), {2: 7})}


def project_kernel(
    groups, ways, tokens, slots, padded, blocks,
    cand_hbm, act_hbm, grad_hbm, win_hbm, wout_hbm,
    own_ref, over_ref, near_ref, far_ref, slot_ref, pick_ref,
    x, w, raw, dealt, cand, rank, start, act_sems, grad_sems, sems,
):
    proj_rank = win_hbm.shape[0]
    features = grad_hbm.shape[1]
    total = x.shape[1]
    examples = cand.shape[1]
    share = examples // ways
    step = x.shape[0] // act_sems.shape[0]
    me = lax.axis_index("tensor")
    home = lax.axis_index("dp")

    def piece(i):
        return pl.ds(pl.multiple_of(i * step, step), step)

    def act_copy(i):
        there = x.at[piece(i), pl.ds(features, total - features)]
        return pltpu.make_async_copy(act_hbm.at[piece(i)], there, act_sems.at[i])

    def grad_copy(i):
        there = x.at[piece(i), pl.ds(0, features)]
        return pltpu.make_async_copy(grad_hbm.at[piece(i)], there, grad_sems.at[i])

    cand_copy = pltpu.make_async_copy(cand_hbm, cand, sems.at[0])
    raw_copy = pltpu.make_async_copy(wout_hbm, raw, sems.at[1])
    there = w.at[pl.ds(proj_rank, proj_rank), pl.ds(features, total - features)]
    win_copy = pltpu.make_async_copy(win_hbm, there, sems.at[2])
    cand_copy.start()
    raw_copy.start()
    win_copy.start()

    @pl.loop(0, act_sems.shape[0])
    def _(i):
        act_copy(i).start()
        grad_copy(i).start()

    cand_copy.wait()

    @pl.loop(0, groups)
    def _(g):
        start[g] = 0

    @pl.loop(0, examples)
    def _(e):
        g = cand[0, e]
        rank[e] = start[g]
        start[g] = start[g] + 1

    def shift(g, below):
        here = start[g]
        start[g] = below
        return below + here

    lax.fori_loop(0, groups, shift, jnp.int32(0))

    half = proj_rank // 2
    r = lax.broadcasted_iota(jnp.int32, (proj_rank, proj_rank), 0)
    c = lax.broadcasted_iota(jnp.int32, (proj_rank, proj_rank), 1)
    pick = (c == jnp.where(r < half, 2 * r, 2 * (r - half) + 1)).astype(jnp.bfloat16)
    raw_copy.wait()
    w[0:proj_rank, 0:features] = jnp.dot(
        pick, raw[...], preferred_element_type=jnp.float32
    ).astype(jnp.bfloat16)
    w[proj_rank:, 0:features] = jnp.zeros((proj_rank, features), w.dtype)
    w[0:proj_rank, features:] = jnp.zeros((proj_rank, total - features), w.dtype)
    win_copy.wait()

    done = 0
    for count, rows in blocks:

        @pl.loop(0, count)
        def _(i, done=done, rows=rows):
            for j in range(rows // step):
                act_copy(done // step + i * (rows // step) + j).wait()
                grad_copy(done // step + i * (rows // step) + j).wait()
            at = pl.multiple_of(done + i * rows, step)
            here = pl.ds(at, rows)
            both = lax.dot_general(x[here, :], w[...], NT, preferred_element_type=jnp.float32)
            first = done // tokens + i * (rows // tokens)
            for k in range(rows // tokens):
                e = first + k
                g = cand[0, e]
                place = start[g] + rank[e]
                owner = place & (ways - 1)
                turn = place >> (ways.bit_length() - 1)
                before = (start[g] + ways - 1 - owner) >> (ways.bit_length() - 1)
                rel = owner ^ me
                slot_ref[rel * share + turn] = (g ^ home) * slots + turn - before
                pick_ref[0, e] = g * padded + rel * slots + turn - before
                row = (rel * share + turn) * tokens
                dealt[pl.ds(pl.multiple_of(row, 8), tokens), :] = both[
                    k * tokens : (k + 1) * tokens
                ]

        done += count * rows

    size = share * tokens
    for r, ref in enumerate((own_ref, near_ref, over_ref, far_ref)):
        ref[...] = dealt[r * size : (r + 1) * size, :]


def project(cands, act, grad, win, wout, tokens, groups, ways, slots, padded):
    examples = cands.shape[1]
    rows = act.shape[0]
    pieces = 8
    step = rows // pieces
    blocks = ((2, step), (3, 2 * step))
    share = rows // ways
    hbm = pl.BlockSpec(memory_space=pltpu.HBM)
    vmem = pl.BlockSpec(memory_space=pltpu.VMEM)
    return pl.pallas_call(
        functools.partial(project_kernel, groups, ways, tokens, slots, padded, blocks),
        in_specs=[hbm] * 5,
        out_specs=[vmem] * 4 + [pl.BlockSpec(memory_space=pltpu.SMEM)] * 2,
        out_shape=[pltpu.VMEM((share, LANES), jnp.float32)] * 4
        + [
            pltpu.SMEM((examples,), jnp.int32),
            jax.ShapeDtypeStruct((1, examples), jnp.int32),
        ],
        scratch_shapes=[
            pltpu.VMEM((rows, act.shape[1] + grad.shape[1]), jnp.bfloat16),
            pltpu.VMEM((2 * win.shape[0], act.shape[1] + grad.shape[1]), jnp.bfloat16),
            pltpu.VMEM(wout.shape, jnp.bfloat16),
            pltpu.VMEM((rows, LANES), jnp.float32),
            pltpu.SMEM((1, examples), jnp.int32),
            pltpu.SMEM((examples,), jnp.int32),
            pltpu.SMEM((groups,), jnp.int32),
            pltpu.SemaphoreType.DMA((pieces,)),
            pltpu.SemaphoreType.DMA((pieces,)),
            pltpu.SemaphoreType.DMA((3,)),
        ],
        compiler_params=pltpu.CompilerParams(vmem_limit_bytes=61 << 20),
        cost_estimate=pl.CostEstimate(
            flops=2 * rows * (act.shape[1] + grad.shape[1]) * 64,
            bytes_accessed=2 * rows * (act.shape[1] + grad.shape[1]),
            transcendentals=0,
        ),
        name="project",
    )(cands, act, grad, win, wout)


def own_kernel(slot_ref, a_ref, b_ref, q_hbm, out_slot_ref, out_ref, held_ref, sems):
    parts = sems.shape[0]
    rows = held_ref.shape[0] // parts

    def load(k):
        here = pl.ds(k * rows, rows)
        return pltpu.make_async_copy(q_hbm.at[here], held_ref.at[here], sems.at[k])

    for k in range(parts):
        load(k).start()
    out_ref[...] = a_ref[...] + b_ref[...]

    @pl.loop(0, out_slot_ref.shape[0])
    def _(i):
        out_slot_ref[i] = slot_ref[i]

    for k in range(parts):
        load(k).wait()


def own_sum(slots, a, b, queries, count):
    smem = pl.BlockSpec(memory_space=pltpu.SMEM)
    vmem = pl.BlockSpec(memory_space=pltpu.VMEM)
    parts = 4 if queries.shape[0] % 64 == 0 else 1
    return pl.pallas_call(
        own_kernel,
        in_specs=[smem, vmem, vmem, pl.BlockSpec(memory_space=pltpu.HBM)],
        out_specs=[smem, vmem, vmem],
        out_shape=[
            pltpu.SMEM((count,), jnp.int32),
            pltpu.VMEM(a.shape, a.dtype),
            pltpu.VMEM(queries.shape, queries.dtype),
        ],
        scratch_shapes=[pltpu.SemaphoreType.DMA((parts,))],
        compiler_params=pltpu.CompilerParams(vmem_limit_bytes=48 << 20),
        cost_estimate=pl.CostEstimate(
            flops=a.size, bytes_accessed=2 * queries.size, transcendentals=0
        ),
        name="own_sum",
    )(slots, a, b, queries)


def unit_kernel(tokens, chunks, row_ref, a_ref, b_ref, *rest):
    out_refs, total, units = rest[:-2], rest[-2], rest[-1]
    total[...] = a_ref[...] + b_ref[...]
    units[...] = jnp.zeros_like(units)
    count = total.shape[0] // tokens
    half = LANES // 2
    width = chunks * LANES
    low = lax.broadcasted_iota(jnp.int32, (chunks, LANES), 1) < half
    low_t = lax.broadcasted_iota(jnp.int32, (tokens, LANES), 1) < half

    @pl.loop(0, count, unroll=16)
    def _(i):
        part = total[pl.ds(pl.multiple_of(i * tokens, 8), tokens), :]
        twice = jnp.where(low_t, pltpu.roll(part, half, 1), part)
        g_hi = part.astype(jnp.bfloat16).astype(jnp.float32)
        a_hi = twice.astype(jnp.bfloat16).astype(jnp.float32)
        left = jnp.concatenate([g_hi, g_hi, part - g_hi], axis=0)[:, :half].astype(jnp.bfloat16)
        right = jnp.concatenate([a_hi, twice - a_hi, a_hi], axis=0).astype(jnp.bfloat16)
        prod = lax.dot_general(left, right, TN, preferred_element_type=jnp.float32)
        entries = jnp.where(low, prod[:chunks], prod[chunks : 2 * chunks])
        square = jnp.sum(entries * entries, axis=0, keepdims=True)
        mean = jnp.sum(square, axis=1, keepdims=True) / width
        unit = (entries * lax.rsqrt(mean + epsilon)).astype(jnp.bfloat16)
        row = pl.multiple_of(row_ref[i] * chunks, chunks)
        units[pl.ds(row, chunks), :] = unit

    for n, ref in enumerate(out_refs):
        size = ref.shape[0]
        ref[...] = units[n * size : (n + 1) * size, :]


def unit_grads(slots, a, b, tokens, chunks, groups, slot_count):
    rows = slot_count * chunks
    whole = pl.BlockSpec(memory_space=pltpu.VMEM)
    return pl.pallas_call(
        functools.partial(unit_kernel, tokens, chunks),
        in_specs=[pl.BlockSpec(memory_space=pltpu.SMEM), whole, whole],
        out_specs=[whole] * groups,
        out_shape=[pltpu.VMEM((rows, LANES), jnp.bfloat16)] * groups,
        scratch_shapes=[
            pltpu.VMEM(a.shape, jnp.float32),
            pltpu.VMEM((groups * rows, LANES), jnp.bfloat16),
        ],
        compiler_params=pltpu.CompilerParams(vmem_limit_bytes=16 << 20),
        cost_estimate=pl.CostEstimate(flops=20_000_000, bytes_accessed=1_000_000, transcendentals=0),
        name="unit_grads",
    )(slots, a, b)


def stage_units(refs, parcels, stage, groups):
    span = stage.shape[0] // (len(refs) // len(parcels) * groups)
    home = lax.axis_index("dp")
    for n, ref in enumerate(refs):
        for i, distance in enumerate(parcels[n % len(parcels)]):
            block = n // len(parcels) * groups + (distance ^ home)
            here = pl.ds(pl.multiple_of(block * span, span), span)
            stage[here, :] = ref[i * span : (i + 1) * span, :].astype(jnp.float32)


def staged_rows(stage, units, at):
    rows = units.shape[0] - at
    chunks = units.shape[1] // LANES
    for j in range(chunks):
        piece = stage[pl.ds(j, rows, stride=chunks), :]
        units[at:, j * LANES : (j + 1) * LANES] = piece.astype(jnp.bfloat16)


def stage_kernel(groups, parcels, *rest):
    refs, (out_ref, stage) = rest[:-2], rest[-2:]
    stage_units(refs, parcels, stage, groups)
    staged_rows(stage, out_ref, 0)


def staged(units, parcels, groups, slots):
    rows = 2 * groups * slots
    width = sum(x.size for x in units) // rows
    vmem = pl.BlockSpec(memory_space=pltpu.VMEM)
    return pl.pallas_call(
        functools.partial(stage_kernel, groups, parcels),
        in_specs=[vmem] * len(units),
        out_specs=vmem,
        out_shape=pltpu.VMEM((rows, width), jnp.bfloat16),
        scratch_shapes=[pltpu.VMEM((rows * width // LANES, LANES), jnp.float32)],
        compiler_params=pltpu.CompilerParams(vmem_limit_bytes=16 << 20),
        cost_estimate=pl.CostEstimate(
            flops=rows * width, bytes_accessed=8 * rows * width, transcendentals=0
        ),
        name="staged",
    )(*units)


def score_kernel(groups, slots, padded, parcels, *rest):
    refs, (early_ref, q_ref, out_ref, stage, units) = rest[:-5], rest[-5:]
    half = groups * slots
    stage_units(refs, parcels, stage, groups)
    units[0 : 2 * half, :] = early_ref[...]
    staged_rows(stage, units, 2 * half)
    total = lax.dot_general(q_ref[...], units[...], NT, preferred_element_type=jnp.float32)

    row = lax.broadcasted_iota(jnp.int32, (groups * padded, 4 * half), 0)
    column = lax.broadcasted_iota(jnp.int32, (1, 4 * half), 1)
    place = column
    for n in range(1, 4):
        place += jnp.where(column >= n * half, slots - half, 0)
    for n in range(4):
        for d in range(1, groups):
            after = (column >= n * half + d * slots) & (column < (n + 1) * half)
            place += jnp.where(after, padded - slots, 0)
    pick = jnp.where(row == place, 1.0, 0.0).astype(jnp.bfloat16)
    out = lax.dot_general(
        pick, total.astype(jnp.bfloat16), NT, preferred_element_type=jnp.float32
    )
    out_ref[...] = out.astype(out_ref.dtype)


def scores_of(late, early, queries, parcels, groups, slots, padded):
    count, width = queries.shape
    half = groups * slots
    vmem = pl.BlockSpec(memory_space=pltpu.VMEM)
    return pl.pallas_call(
        functools.partial(score_kernel, groups, slots, padded, parcels),
        in_specs=[vmem] * (len(late) + 2),
        out_specs=vmem,
        out_shape=pltpu.VMEM((groups * padded, count), jnp.bfloat16),
        scratch_shapes=[
            pltpu.VMEM((2 * half * width // LANES, LANES), jnp.float32),
            pltpu.VMEM((4 * half, width), jnp.bfloat16),
        ],
        compiler_params=pltpu.CompilerParams(vmem_limit_bytes=24 << 20),
        cost_estimate=pl.CostEstimate(
            flops=2 * 4 * half * queries.size, bytes_accessed=2 * queries.size, transcendentals=0
        ),
        name="scores",
    )(*late, early, queries)


def pick_kernel(row_ref, x_ref, out_ref):
    count = row_ref.shape[1]
    rows = x_ref.shape[0]
    parts = x_ref.shape[1] // LANES
    hit = lax.broadcasted_iota(jnp.int32, (rows, count), 0) == row_ref[...]
    pick = jnp.where(hit, 1.0, 0.0).T.astype(jnp.bfloat16)
    got = jnp.dot(pick, x_ref[...], preferred_element_type=jnp.float32)
    for j in range(parts):
        out_ref[pl.ds(j, count, stride=parts), :] = got[:, j * LANES : (j + 1) * LANES]


def pick_rows(row, x):
    vmem = pl.BlockSpec(memory_space=pltpu.VMEM)
    count, width = row.shape[1], x.shape[1]
    return pl.pallas_call(
        pick_kernel,
        in_specs=[vmem, vmem],
        out_specs=vmem,
        out_shape=jax.ShapeDtypeStruct((count * (width // LANES), LANES), jnp.float32),
        compiler_params=pltpu.CompilerParams(vmem_limit_bytes=16 << 20),
        cost_estimate=pl.CostEstimate(flops=16_000_000, bytes_accessed=400_000, transcendentals=0),
        name="pick_rows",
    )(row, x)


def local_one(activations, out_grads, proj_in, proj_out, queries, candidates):
    examples, tokens, hidden = activations.shape
    features = out_grads.shape[2]
    groups = lax.axis_size("dp")
    ways = lax.axis_size("tensor")
    capacity = max(2, 5 * examples // (2 * groups))
    slots = -(-capacity // ways)
    padded = -(-ways * slots // 8) * 8
    query_block = queries[0]
    chunks = query_block.shape[1] // LANES
    core = [(i, i ^ 1) for i in range(ways)]
    across = [(i, i ^ 2) for i in range(ways)]

    own_part, over_part, near_part, far_part, my_slots, pick = project(
        candidates.reshape(1, examples),
        activations.reshape(examples * tokens, hidden),
        out_grads.reshape(examples * tokens, features),
        proj_in.T,
        proj_out.T,
        tokens,
        groups,
        ways,
        slots,
        padded,
    )
    far_in = lax.ppermute(far_part, "tensor", core)
    near_in = lax.ppermute(near_part, "tensor", core)
    across_in = lax.ppermute(over_part + far_in, "tensor", across)

    here_slots, here, held = own_sum(
        my_slots, own_part, near_in, query_block, examples // ways
    )
    units = unit_grads(here_slots, here, across_in, tokens, chunks, groups, slots)
    parcels, after = PLANS[groups]
    arrived = [units[0]] + [None] * (groups - 1)
    for k in (k for parcel in parcels for k in parcel if k):
        block = units[k]
        if k in after:
            block, _ = lax.optimization_barrier((block, arrived[after[k]]))
        arrived[k] = lax.ppermute(block, "dp", [(i, i ^ k) for i in range(groups)])
    own = [jnp.concatenate([arrived[k] for k in parcel], axis=0) for parcel in parcels]
    over_y = [lax.ppermute(x, "tensor", across) for x in own]
    over_core = [lax.ppermute(x, "tensor", core) for x in own]
    early = staged(own + over_core, parcels, groups, slots)
    over_both = [lax.ppermute(x, "tensor", core) for x in over_y]
    both = scores_of(over_y + over_both, early, held, parcels, groups, slots, padded)
    block = both.reshape(groups, padded, both.shape[1])
    returned = lax.all_to_all(block, "dp", split_axis=0, concat_axis=0, tiled=True)
    picked = pick_rows(pick, returned.reshape(both.shape))
    return picked.reshape(examples, 1, both.shape[1])


def local_many(activations, out_grads, proj_in, proj_out, queries, candidates):
    examples_here, tokens_here, hidden_here = activations.shape
    proj_rank = proj_in.shape[1]
    per_example = candidates.shape[1]
    groups = lax.axis_size("dp")
    capacity = max(2, 5 * examples_here * per_example // (2 * groups))
    act_proj = jnp.dot(
        activations.reshape(examples_here * tokens_here, hidden_here),
        proj_in,
        preferred_element_type=jnp.float32,
    )
    grad_proj = jnp.dot(
        out_grads.reshape(examples_here * tokens_here, out_grads.shape[2]),
        proj_out,
        preferred_element_type=jnp.float32,
    )
    both_proj = jnp.concatenate([grad_proj, act_proj], axis=1).reshape(
        examples_here, tokens_here, 2 * proj_rank
    )
    summed = lax.psum(both_proj, "tensor")
    grad_side = summed[:, :, :proj_rank]
    act_side = summed[:, :, proj_rank:]
    example_grads = jnp.einsum(
        "eta,etb->eab", grad_side, act_side, precision=lax.Precision.HIGHEST
    ).reshape(examples_here, proj_rank * proj_rank)
    inv_rms = lax.rsqrt(jnp.mean(example_grads * example_grads, axis=1, keepdims=True) + epsilon)
    unit = (example_grads * inv_rms).astype(jnp.bfloat16)
    flat_cands = candidates.reshape(-1)
    hit_table = (flat_cands[:, None] == jnp.arange(groups, dtype=jnp.int32)[None, :]).astype(
        jnp.int32
    )
    earlier = jnp.cumsum(hit_table, axis=0) - hit_table
    slot_index = jnp.sum(earlier * hit_table, axis=1)
    dest_index = flat_cands * capacity + slot_index
    row_copies = jnp.repeat(unit, per_example, axis=0)
    grad_width = unit.shape[1]
    send_buffer = (
        jnp.zeros((groups * capacity, grad_width), jnp.bfloat16).at[dest_index].set(row_copies)
    )
    send_buffer = send_buffer.reshape(groups, capacity, grad_width)
    col_width = grad_width // lax.axis_size("tensor")
    column_part = lax.dynamic_slice_in_dim(
        send_buffer, lax.axis_index("tensor") * col_width, col_width, 2
    )
    received = lax.all_to_all(column_part, "dp", split_axis=0, concat_axis=0, tiled=True)
    slot_scores = jnp.einsum(
        "gsk,qk->gsq",
        lax.all_gather(received, "tensor", axis=2, tiled=True),
        queries[0],
        preferred_element_type=jnp.float32,
    )
    returned = lax.all_to_all(slot_scores, "dp", split_axis=0, concat_axis=0, tiled=True)
    picked = returned.reshape(groups * capacity, returned.shape[2])[dest_index]
    return picked.reshape(examples_here, per_example, returned.shape[2])


def local(activations, out_grads, proj_in, proj_out, queries, candidates):
    one = candidates.shape[1] == 1 and lax.axis_size("tensor") == 4
    one = one and lax.axis_size("dp") in PLANS
    return (local_one if one else local_many)(
        activations, out_grads, proj_in, proj_out, queries, candidates
    )


def solution(mesh):
    placed = (
        P("dp", None, "tensor"),
        P("dp", None, "tensor"),
        P("tensor", None),
        P("tensor", None),
        P("dp", "tensor", None),
        P("dp", None),
    )
    return jax.shard_map(
        local, mesh=mesh, in_specs=placed, out_specs=P("dp", None, "tensor"), check_vma=False
    )
```
